32 devices in a mesh: dp: 8 (over y, x, core), seq: 4 (over z).
Axes of the slice: x: 2, y: 2, z: 4, core: 2. Of those that a mesh axis runs over, the one named last changes fastest.
Arguments:
- features: bfloat16 [4, 8, 2048, 512], P(None, 'dp', 'seq'), may hold values from -6 to 6
- lengths: int32 [4, 8], P(None, 'dp'), may hold values from 512 to 2048, as said below
- dw_weight: bfloat16 [2, 7, 512], P(None, None, 'dp'), may hold values from -2 to 2
- block_gains: bfloat16 [2, 2, 512], P(None, None, 'dp'), may hold values from 0.5 to 1.5
- block_biases: bfloat16 [2, 3, 512], P(None, None, 'dp'), may hold values from -1.75 to 1.75
- up_weight: bfloat16 [2, 512, 1536], P(None, 'dp'), may hold values from -0.25 to 0.25
- up_bias: bfloat16 [2, 1536], P(None, 'dp'), may hold values from -1.75 to 1.75
- down_weight: bfloat16 [2, 1536, 512], P(None, 'dp'), may hold values from -0.15625 to 0.15625
- head_gain: float32 [512], P('dp'), may hold values from 0.5 to 1.5
- head_shift: float32 [512], P('dp'), may hold values from -1.75 to 1.75
- head_weight: float32 [512, 1026], P('dp'), may hold values from -0.25 to 0.25
- head_bias: float32 [1026], replicated
- audio_grad: float32 [4, 8, 2048, 256], P(None, 'dp', 'seq'), may hold values from -6 to 6
Outputs:
- audio: float32 [4, 8, 2048, 256], P(None, 'dp', 'seq')
- feature_grad: float32 [4, 8, 2048, 512], P(None, 'dp', 'seq')
- dw_grad: float32 [2, 7, 512], P(None, None, 'dp')
- gains_grad: float32 [2, 2, 512], P(None, None, 'dp')
- biases_grad: float32 [2, 3, 512], P(None, None, 'dp')
- up_grad: float32 [2, 512, 1536], P(None, 'dp')
- up_bias_grad: float32 [2, 1536], P(None, 'dp')
- down_grad: float32 [2, 1536, 512], P(None, 'dp')
- head_gain_grad: float32 [512], P('dp')
- head_shift_grad: float32 [512], P('dp')
- head_weight_grad: float32 [512, 1026], P('dp')
- head_bias_grad: float32 [1026], replicated
The draws below stay inside these ranges and needn't reach their ends.
Inputs may be any that keep to these rules, and one draw needn't show every extreme that they name: `lengths`: some utterance of each draw fills all 2048 frames.
All inputs are finite; a program needn't handle non-finite values.
Results may differ from the reference program's by a relative error of at most 0.018.
Values may be sent and summed in bfloat16 or wider, within the bound.
No kernel may reach another device: no remote copies, remote signals or barrier semaphores. Data moves between devices by JAX's collectives and lax.ppermute only.
A program may use at most 168 MiB of HBM per device.

```python
import math
import jax
import jax.numpy as jnp
from jax import lax

D = 512
FF = 1536
NFFT = 1024
HOP = 256
BINS = 513
KERNEL = 7
BLOCKS = 2
MICRO = 4
SEQS = 8
FRAMES = 2048


def draw_lengths(key, part):
    values = jax.random.randint(key, (MICRO, SEQS), FRAMES // 4, FRAMES + 1, dtype=jnp.int32)
    return values.at[0, 0].set(FRAMES)


def draw_head_bias(key, part):
    first_key, second_key = jax.random.split(jax.random.fold_in(key, 7))
    log_part = 0.5 + 0.3 * jax.random.normal(first_key, (BINS,), jnp.float32)
    phase_part = 0.3 * jax.random.normal(second_key, (BINS,), jnp.float32)
    return jnp.concatenate([log_part, phase_part]).astype(jnp.float32)


def steps_of(stream_key, extent, shards, smallest, largest):
    def one(axis_at, blocks):
        steps = jax.random.uniform(jax.random.fold_in(jax.random.fold_in(stream_key, 6), axis_at), (blocks,), jnp.float32, smallest / len(shards), largest / len(shards))
        return jnp.repeat(jnp.exp(steps), extent[axis_at] // blocks).reshape((-1,) + (1,) * (len(extent) - axis_at - 1))

    loudness = one(*shards[0])
    for cut in shards[1:]:
        loudness = loudness * one(*cut)
    return loudness


def normal_values(stream_key, extent, spread, most, cuts=(), kind=jnp.bfloat16):
    values = spread * jax.random.normal(stream_key, extent, jnp.float32)
    if cuts:
        values = values * steps_of(stream_key, extent, cuts, -0.22, 0.18)
    return jnp.clip(values, -most, most).astype(kind)


def setup_inputs(seed: int = 0) -> dict:
    keys = jax.random.split(jax.random.key(seed), 14)
    features = normal_values(keys[0], (MICRO, SEQS, FRAMES, D), 1.0, 6.0, ((1, 8), (2, 4)))
    lengths = draw_lengths(jax.random.fold_in(keys[13], 71), 0)
    dw_weight = normal_values(keys[2], (BLOCKS, KERNEL, D), KERNEL ** -0.5, 2.0, ((2, 8),))
    block_gains = jnp.clip(1.0 + 0.1 * jax.random.normal(keys[3], (BLOCKS, 2, D), jnp.float32), 0.5, 1.5).astype(jnp.bfloat16)
    block_biases = normal_values(keys[4], (BLOCKS, 3, D), 0.3, 1.75, ((2, 8),))
    up_weight = normal_values(keys[5], (BLOCKS, D, FF), D ** -0.5, 0.25, ((1, 8),))
    up_bias = normal_values(keys[6], (BLOCKS, FF), 0.3, 1.75, ((1, 8),))
    down_weight = normal_values(keys[7], (BLOCKS, FF, D), FF ** -0.5, 0.15625, ((1, 8),))
    head_gain = jnp.clip(1.0 + 0.1 * jax.random.normal(keys[8], (D,), jnp.float32), 0.5, 1.5)
    head_shift = normal_values(keys[9], (D,), 0.3, 1.75, ((0, 8),), jnp.float32)
    head_weight = normal_values(keys[10], (D, 2 * BINS), D ** -0.5, 0.25, ((0, 8),), jnp.float32)
    head_bias = draw_head_bias(jax.random.fold_in(keys[13], 71), 0)
    audio_grad = normal_values(keys[12], (MICRO, SEQS, FRAMES, HOP), 1.0, 6.0, ((1, 8), (2, 4)), jnp.float32)
    return {"features": features, "lengths": lengths, "dw_weight": dw_weight, "block_gains": block_gains, "block_biases": block_biases, "up_weight": up_weight, "up_bias": up_bias, "down_weight": down_weight, "head_gain": head_gain, "head_shift": head_shift, "head_weight": head_weight, "head_bias": head_bias, "audio_grad": audio_grad}


exact_mode = lax.Precision.HIGHEST
norm_eps = 1e-06

@jax.custom_vjp
def low(v):
    return lax.optimization_barrier(v.astype(jnp.bfloat16)).astype(jnp.float32)

@jax.custom_vjp
def low_back(v):
    return v

def low_keep(v):
    return (low(v), None)

def low_pass(kept, grad):
    return (grad,)

def back_keep(v):
    return (v, None)

def back_low(kept, grad):
    return (low(grad),)
low.defvjp(low_keep, low_pass)
low_back.defvjp(back_keep, back_low)

def layer_norm(values, norm_gain, norm_shift):
    row_mean = lax.optimization_barrier(jnp.mean(values, axis=-1, keepdims=True))
    centred = values - row_mean
    variance = lax.optimization_barrier(jnp.mean(centred * centred, axis=-1, keepdims=True))
    return centred * lax.rsqrt(variance + norm_eps) * norm_gain + norm_shift

def dft_tables():
    frequency = jnp.arange(BINS, dtype=jnp.int32)
    sample = jnp.arange(NFFT, dtype=jnp.int32)
    product = frequency[:, None] * sample[None, :] % NFFT
    angles = product.astype(jnp.float32) * (2.0 * math.pi / NFFT)
    edge = (frequency == 0) | (frequency == NFFT // 2)
    weight_row = jnp.where(edge, 1.0, 2.0).astype(jnp.float32) / NFFT
    return (jnp.cos(angles) * weight_row[:, None], -jnp.sin(angles) * weight_row[:, None])

def hann_window():
    sample = jnp.arange(NFFT, dtype=jnp.int32).astype(jnp.float32)
    return 0.5 - 0.5 * jnp.cos(sample * (2.0 * math.pi / NFFT))

def intersection_add(framed):
    summed = jnp.zeros((framed.shape[0] + 3, HOP), jnp.float32)
    for q in range(4):
        quarter = framed[:, q * HOP:(q + 1) * HOP]
        summed = summed + jnp.pad(quarter, ((q, 3 - q), (0, 0)))
    return summed

def one_sequence(params, sequence, seq_len):
    dw_all, gains_all, biases_all, up_all, upb_all, down_all, head_gain, head_shift, head_weight, head_bias = params
    positions = jnp.arange(FRAMES, dtype=jnp.int32)
    frame_mask = (positions < seq_len).astype(jnp.float32)[:, None]
    hidden = sequence * frame_mask
    for convnext_block in range(BLOCKS):
        block_in = low(hidden)
        padded = jnp.pad(block_in, ((3, 3), (0, 0)))
        conv_out = biases_all[convnext_block, 0]
        for k in range(KERNEL):
            conv_out = conv_out + dw_all[convnext_block, k] * padded[k:k + FRAMES]
        conv_out = low_back(conv_out)
        normed_low = low(layer_norm(conv_out, gains_all[convnext_block, 0], biases_all[convnext_block, 1]))
        pre_act = low_back(jnp.dot(normed_low, up_all[convnext_block], precision=exact_mode) + upb_all[convnext_block])
        act_low = low(jax.nn.gelu(pre_act, approximate=False))
        branch = low_back(jnp.dot(act_low, down_all[convnext_block], precision=exact_mode) + biases_all[convnext_block, 2])
        hidden = hidden + gains_all[convnext_block, 1] * branch
    normed = layer_norm(hidden, head_gain, head_shift)
    logits = jnp.dot(normed, head_weight, precision=exact_mode) + head_bias
    magnitude = jnp.exp(logits[:, :BINS])
    phase = logits[:, BINS:]
    cos_table, sin_table = dft_tables()
    window = hann_window()
    framed = jnp.dot(magnitude * jnp.cos(phase), cos_table, precision=exact_mode)
    framed = (framed + jnp.dot(magnitude * jnp.sin(phase), sin_table, precision=exact_mode)) * window
    summed = intersection_add(framed)[2:FRAMES + 2]
    squares = jnp.broadcast_to(window * window, (FRAMES, NFFT))
    envelope = intersection_add(squares)[2:FRAMES + 2]
    return summed / envelope * frame_mask

def reference(features, lengths, dw_weight, block_gains, block_biases, up_weight, up_bias, down_weight, head_gain, head_shift, head_weight, head_bias, audio_grad):
    params = (dw_weight.astype(jnp.float32), block_gains.astype(jnp.float32), block_biases.astype(jnp.float32), up_weight.astype(jnp.float32), up_bias.astype(jnp.float32), down_weight.astype(jnp.float32), head_gain, head_shift, head_weight, head_bias)
    sequences = features.astype(jnp.float32).reshape(MICRO * SEQS, FRAMES, D)
    seq_lens = lengths.reshape(MICRO * SEQS).astype(jnp.int32)
    cotangent = audio_grad.reshape(MICRO * SEQS, FRAMES, HOP)
    checked = jax.checkpoint(one_sequence)

    def whole(param_set, inputs):

        def step(carry, item):
            return (carry, checked(param_set, item[0], item[1]))
        unused, result = lax.scan(step, jnp.zeros((), jnp.float32), (inputs, seq_lens))
        return result
    audio, pullback = jax.vjp(whole, params, sequences)
    param_grads, input_grads = pullback(cotangent)
    return (audio.reshape(MICRO, SEQS, FRAMES, HOP), input_grads.reshape(MICRO, SEQS, FRAMES, D), param_grads[0], param_grads[1], param_grads[2], param_grads[3], param_grads[4], param_grads[5], param_grads[6], param_grads[7], param_grads[8], param_grads[9])
```

```python
import functools
import math

import jax
import jax.numpy as jnp
import numpy as np
from jax import lax
from jax.experimental import pallas as pl
from jax.experimental.pallas import tpu as pltpu
from jax.sharding import PartitionSpec as P

NFFT = 1024
HOP = 256
BINS = 513
HALF = 512
EXTRA = 128
KERNEL = 7
BLOCKS = 2
HALO = 16
norm_eps = 1e-06
f32 = jnp.float32
low = jnp.bfloat16
rows_dims = (((0,), (0,)), ((), ()))
cols_dims = (((1,), (1,)), ((), ()))
MiB = 2**20
GELU = (0.7978202661111929, 0.03654664812915587, -0.00019444764679970054, -1.3688682486738934e-05)
SIN = (6.283184921107194, -41.34159015596926, 81.59997289449204, -76.61480381354174, 41.34439732745281, -12.473668162531846)
COS = (0.9999992215705861, -19.738982516102407, 64.92872660899411, -85.27239689575316, 58.79403819232432, -21.076781286284348)


def window_values():
    return 0.5 - 0.5 * np.cos(np.arange(NFFT) * (2.0 * math.pi / NFFT))


def head_tables():
    row = np.arange(NFFT)
    frequency = np.where(row < HALF, row, np.where(row == HALF, HALF, row - HALF))
    angles = (frequency[:, None] * np.arange(NFFT)[None, :] % NFFT) * (2.0 * math.pi / NFFT)
    weight = np.where((row == 0) | (row == HALF), 1.0, 2.0)[:, None] / NFFT
    values = np.where((row <= HALF)[:, None], np.cos(angles), -np.sin(angles)) * weight
    return (values * window_values()[None, :]).astype(jnp.bfloat16)


def swap(x, axis, d):
    return lax.ppermute(x, axis, [(i, i ^ d) for i in range(lax.axis_size(axis))])


def by_owner(pieces, axis):
    me = lax.axis_index(axis)
    stacked = jnp.stack(pieces) if isinstance(pieces, list) else pieces
    count = stacked.shape[0]
    bit = 1
    while bit < count:
        split = stacked.reshape((count // (2 * bit), 2, bit) + stacked.shape[1:])
        split = jnp.where((me & bit) != 0, split[:, ::-1], split)
        stacked = split.reshape(stacked.shape)
        bit *= 2
    return stacked


def gathered(x):
    even = jnp.stack([x] + [swap(x, "dp", d) for d in range(2, lax.axis_size("dp"), 2)])
    return even, swap(even, "dp", 1)


def poly(z, coefficients):
    p = coefficients[-1]
    for c in coefficients[-2::-1]:
        p = p * z + c
    return p


def gelu_parts(x):
    u = jnp.clip(x, -5.2, 5.2)
    z = u * u
    p = poly(z, [jnp.asarray(c, x.dtype) for c in GELU])
    half = jnp.asarray(0.5, x.dtype)
    cumulative = half * jnp.tanh(u * p) + half
    density = jnp.exp2(z * jnp.asarray(-0.5 * math.log2(math.e), x.dtype))
    return x * cumulative, cumulative + (x * jnp.asarray(1.0 / math.sqrt(2.0 * math.pi), x.dtype)) * density


def norm_parts(values):
    centred = values - jnp.mean(values, axis=1, keepdims=True)
    inv_std = lax.rsqrt(jnp.mean(centred * centred, axis=1, keepdims=True) + norm_eps)
    return centred * inv_std, inv_std


def norm_back(normed_grad, unit, inv_std, gain):
    unit_grad = normed_grad * gain
    inner = jnp.mean(unit_grad * unit, axis=1, keepdims=True)
    return inv_std * (unit_grad - jnp.mean(unit_grad, axis=1, keepdims=True) - unit * inner)


def frames_of(scal, ext):
    t = lax.broadcasted_iota(jnp.int32, (ext, 1), 0) + scal[0]
    return t, (t >= 0) & (t < scal[1])


def total_rows(x):
    return jnp.sum(x, axis=0, keepdims=True)


def assemble(scal, even_ref, odd_ref, whole_ref, sems):
    size = even_ref.shape[1]
    copies = []
    for h in range(even_ref.shape[0]):
        for c, ref in enumerate((even_ref, odd_ref)):
            at = pl.multiple_of((scal[2] ^ (2 * h + c)) * size, size)
            copies.append(pltpu.make_async_copy(ref.at[h], whole_ref.at[pl.ds(at, size)], sems.at[2 * h + c]))
    for copy in copies:
        copy.start()
    return copies


def split_out(scal, total_ref, keep_ref, send_ref):
    size = keep_ref.shape[1]
    for h in range(keep_ref.shape[0]):
        at = pl.multiple_of((scal[2] ^ (2 * h)) * size, size)
        keep_ref[h] = total_ref[pl.ds(at, size), :]
        at = pl.multiple_of((scal[2] ^ (2 * h + 1)) * size, size)
        send_ref[h] = total_ref[pl.ds(at, size), :].astype(low)


def call(kernel, grid, scal, ins, outs, scratch, flops, name):
    def spec(shape, kind):
        if kind == "any":
            return pl.BlockSpec(memory_space=pl.ANY)
        if kind == "rows":
            return pl.BlockSpec((1,) + tuple(shape[1:]), lambda i, s: (i,) + (0,) * (len(shape) - 1))
        return pl.BlockSpec(tuple(shape), lambda i, s: (0,) * len(shape))

    moved = sum(a.size * a.dtype.itemsize for a, _ in ins)
    moved += sum(math.prod(s) * jnp.dtype(d).itemsize for s, d, _ in outs)
    return pl.pallas_call(
        kernel,
        out_shape=[jax.ShapeDtypeStruct(tuple(s), d) for s, d, _ in outs],
        grid_spec=pltpu.PrefetchScalarGridSpec(
            num_scalar_prefetch=1,
            grid=(grid,),
            in_specs=[spec(a.shape, kind) for a, kind in ins],
            out_specs=[spec(s, kind) for s, _, kind in outs],
            scratch_shapes=scratch,
        ),
        compiler_params=pltpu.CompilerParams(vmem_limit_bytes=56 * MiB, dimension_semantics=("arbitrary",)),
        cost_estimate=pl.CostEstimate(flops=int(flops), bytes_accessed=int(moved), transcendentals=0),
        name=name,
    )(scal, *[a for a, _ in ins])


def dft_kernel(ext, scal, grad_ref, recip_ref, table_ref, out_ref):
    t, inside = frames_of(scal, ext)
    mask = inside & (t < scal[3 + pl.program_id(0)])
    own = jnp.where(mask, grad_ref[0] * recip_ref[...], 0.0)
    parts = [own if q == 2 else pltpu.roll(own, (2 - q) % ext, 0) for q in range(4)]
    framed = jnp.where(inside, jnp.concatenate(parts, axis=1), 0.0).astype(low)
    out_ref[0] = lax.dot_general(framed, table_ref[...], cols_dims, preferred_element_type=f32).astype(low)


def conv_forward(block_in, taps_ref, bias):
    ext = block_in.shape[0]
    conv = bias + taps_ref[3:4] * block_in
    for k in range(KERNEL):
        if k != 3:
            conv = conv + taps_ref[k : k + 1] * pltpu.roll(block_in, (3 - k) % ext, 0)
    return conv


def conv_kernel(ext, scal, features_ref, taps_ref, vec_ref, normed_ref, unit_ref, inv_ref):
    t, inside = frames_of(scal, ext)
    h = jnp.where(inside & (t < scal[3 + pl.program_id(0)]), features_ref[0].astype(f32), 0.0)
    unit, inv_std = norm_parts(conv_forward(h, taps_ref, vec_ref[2:3]))
    unit_ref[0] = unit.astype(low)
    inv_ref[0] = inv_std
    normed_ref[0] = (unit * vec_ref[0:1] + vec_ref[3:4]).astype(low)


def up_kernel(chunk, scal, normed_ref, bias_ref, even_ref, odd_ref, act_ref, slope_ref, weight_ref, sems):
    @pl.when(pl.program_id(0) == 0)
    def _():
        for copy in assemble(scal, even_ref, odd_ref, weight_ref, sems):
            copy.wait()

    normed = normed_ref[0]
    for c in range(0, weight_ref.shape[1], chunk):
        pre = jnp.dot(normed, weight_ref[:, c : c + chunk], preferred_element_type=f32) + bias_ref[:, c : c + chunk]
        act, slope = gelu_parts(pre.astype(low))
        act_ref[0, :, c : c + chunk] = act
        slope_ref[0, :, c : c + chunk] = slope


def down_kernel(ext, first, final, scal, act_ref, h_ref, vec_ref, taps_ref, next_ref, even_ref, odd_ref, *refs):
    if final:
        hidden_ref, branch_ref, weight_ref, sems = refs
    else:
        hidden_ref, branch_ref, normed_ref, unit_ref, inv_ref, weight_ref, sems = refs

    @pl.when(pl.program_id(0) == 0)
    def _():
        for copy in assemble(scal, even_ref, odd_ref, weight_ref, sems):
            copy.wait()

    t, inside = frames_of(scal, ext)
    h = h_ref[0].astype(f32)
    if first:
        h = jnp.where(inside & (t < scal[3 + pl.program_id(0)]), h, 0.0)
    branch = jnp.dot(act_ref[0], weight_ref[...], preferred_element_type=f32) + vec_ref[4:5]
    branch_ref[0] = branch.astype(low)
    hidden = h + vec_ref[1:2] * branch
    hidden_ref[0] = hidden
    if not final:
        block_in = jnp.where(inside, hidden, 0.0).astype(low).astype(f32)
        unit, inv_std = norm_parts(conv_forward(block_in, taps_ref, next_ref[2:3]))
        unit_ref[0] = unit.astype(low)
        inv_ref[0] = inv_std
        normed_ref[0] = (unit * next_ref[0:1] + next_ref[3:4]).astype(low)


def head_kernel(
    ext, rows, scal, h_ref, tgrad_ref, recip_ref, table_ref, vec_ref, bias_ref, even_ref, odd_ref,
    audio_ref, hgrad_ref, keep_ref, send_ref, small_ref, sbias_ref, weight_ref, total_ref, sems,
):
    step = pl.program_id(0)

    @pl.when(step == 0)
    def _():
        copies = assemble(scal, even_ref, odd_ref, weight_ref, sems)
        total_ref[...] = jnp.zeros_like(total_ref)
        small_ref[...] = jnp.zeros_like(small_ref)
        sbias_ref[...] = jnp.zeros_like(sbias_ref)
        for copy in copies:
            copy.wait()

    t, inside = frames_of(scal, ext)
    own = slice(HALO, HALO + rows)
    unit, inv_std = norm_parts(h_ref[0])
    normed = (unit * vec_ref[0:1] + vec_ref[1:2]).astype(low)
    logits = jnp.dot(normed, weight_ref[...], preferred_element_type=f32) + bias_ref[...]

    def turns(x):
        r = x * (1.0 / (2.0 * math.pi))
        r = r - jnp.floor(r + 0.5)
        z = r * r
        return poly(z, COS), r * poly(z, SIN)

    magnitude = jnp.exp(logits[:, :HALF])
    cos, sin = turns(logits[:, HALF : 2 * HALF])
    re = magnitude * cos
    im = magnitude * sin
    last = logits[:, 2 * HALF :]
    lane = lax.broadcasted_iota(jnp.int32, (ext, EXTRA), 1)
    cos, sin = turns(pltpu.roll(last, EXTRA - 1, 1))
    top = jnp.exp(jnp.where(lane == 0, last, 0.0))
    top_re = top * cos
    top_im = top * sin
    im_first = jnp.where(lane == 0, top_re, im[:, :EXTRA])
    spectrum = jnp.concatenate([re, im_first, im[:, EXTRA:]], axis=1).astype(low)
    framed = jnp.dot(spectrum, table_ref[...], preferred_element_type=f32)
    framed = jnp.where(inside, framed, 0.0)
    audio = framed[:, 2 * HOP : 3 * HOP]
    for q in (0, 1, 3):
        audio = audio + pltpu.roll(framed[:, q * HOP : (q + 1) * HOP], (q - 2) % ext, 0)
    audio = jnp.where(t < scal[3 + step], audio * recip_ref[...], 0.0)
    audio_ref[0] = audio[own]

    tgrad = tgrad_ref[0].astype(f32)
    re_grad = tgrad[:, :HALF]
    top_grad = tgrad[:, HALF : HALF + EXTRA]
    im_grad = jnp.concatenate([jnp.where(lane == 0, 0.0, top_grad), tgrad[:, HALF + EXTRA :]], axis=1)
    log_last = jnp.where(lane == 0, top_grad * top_re, 0.0)
    phase_last = jnp.where(lane == 1, pltpu.roll(top_grad * top_im, 1, 1), 0.0)
    logit_grad = jnp.concatenate(
        [re_grad * re + im_grad * im, im_grad * re - re_grad * im, log_last - phase_last], axis=1
    )
    sbias_ref[...] += total_rows(logit_grad[own])
    logit_low = logit_grad.astype(low)
    total_ref[...] += lax.dot_general(normed[own], logit_low[own], rows_dims, preferred_element_type=f32)
    normed_grad = lax.dot_general(logit_low, weight_ref[...], cols_dims, preferred_element_type=f32)
    hgrad_ref[0] = norm_back(normed_grad, unit, inv_std, vec_ref[0:1])
    small_ref[0:1] += total_rows((normed_grad * unit)[own])
    small_ref[1:2] += total_rows(normed_grad[own])

    @pl.when(step == pl.num_programs(0) - 1)
    def _():
        split_out(scal, total_ref, keep_ref, send_ref)


def back_down_kernel(
    rows, chunk, scal, hgrad_ref, branch_ref, act_ref, slope_ref, vec_ref, even_ref, odd_ref,
    pgrad_ref, keep_ref, send_ref, small_ref, sbias_ref, weight_ref, total_ref, sems,
):
    step = pl.program_id(0)

    @pl.when(step == 0)
    def _():
        copies = assemble(scal, even_ref, odd_ref, weight_ref, sems)
        total_ref[...] = jnp.zeros_like(total_ref)
        small_ref[...] = jnp.zeros_like(small_ref)
        sbias_ref[...] = jnp.zeros_like(sbias_ref)
        for copy in copies:
            copy.wait()

    own = slice(HALO, HALO + rows)
    hgrad = hgrad_ref[0]
    small_ref[0:1] += total_rows(hgrad[own] * branch_ref[0, own].astype(f32))
    branch_grad = (vec_ref[1:2] * hgrad).astype(low)
    small_ref[1:2] += total_rows(branch_grad[own].astype(f32))
    for c in range(0, weight_ref.shape[0], chunk):
        part = slice(c, c + chunk)
        total_ref[part] += lax.dot_general(act_ref[0, own, part], branch_grad[own], rows_dims, preferred_element_type=f32)
        act_grad = lax.dot_general(branch_grad, weight_ref[part], cols_dims, preferred_element_type=f32)
        pre_grad = (act_grad * slope_ref[0, :, part].astype(f32)).astype(low)
        pgrad_ref[0, :, part] = pre_grad
        sbias_ref[:, part] += total_rows(pre_grad[own].astype(f32))

    @pl.when(step == pl.num_programs(0) - 1)
    def _():
        split_out(scal, total_ref, keep_ref, send_ref)


def up_grad_kernel(rows, scal, normed_ref, pgrad_ref, keep_ref, send_ref, total_ref):
    step = pl.program_id(0)

    @pl.when(step == 0)
    def _():
        total_ref[...] = jnp.zeros_like(total_ref)

    own = slice(HALO, HALO + rows)
    total_ref[...] += lax.dot_general(normed_ref[0, own], pgrad_ref[0, own], rows_dims, preferred_element_type=f32)

    @pl.when(step == pl.num_programs(0) - 1)
    def _():
        split_out(scal, total_ref, keep_ref, send_ref)


def back_up_kernel(
    ext, rows, first, scal, pgrad_ref, unit_ref, inv_ref, block_in_ref, hgrad_ref, vec_ref, taps_ref, even_ref, odd_ref,
    out_ref, small_ref, weight_ref, sems,
):
    step = pl.program_id(0)

    @pl.when(step == 0)
    def _():
        copies = assemble(scal, even_ref, odd_ref, weight_ref, sems)
        small_ref[...] = jnp.zeros_like(small_ref)
        for copy in copies:
            copy.wait()

    t, inside = frames_of(scal, ext)
    mask = inside & (t < scal[3 + step])
    own = slice(HALO, HALO + rows)
    block_in = block_in_ref[0]
    block_in = jnp.where(mask if first else inside, block_in.astype(f32), 0.0)[own]
    if not first:
        block_in = block_in.astype(low).astype(f32)
    unit = unit_ref[0].astype(f32)
    normed_grad = lax.dot_general(pgrad_ref[0], weight_ref[...], cols_dims, preferred_element_type=f32)
    small_ref[8:9] += total_rows((normed_grad * unit)[own])
    small_ref[9:10] += total_rows(normed_grad[own])
    conv_grad = norm_back(normed_grad, unit, inv_ref[0], vec_ref[0:1])
    conv_grad = jnp.where(inside, conv_grad, 0.0).astype(low).astype(f32)
    small_ref[7:8] += total_rows(conv_grad[own])
    hgrad = hgrad_ref[0]
    for k in range(KERNEL):
        moved = conv_grad if k == 3 else pltpu.roll(conv_grad, (k - 3) % ext, 0)
        hgrad = hgrad + taps_ref[k : k + 1] * moved
        small_ref[k : k + 1] += total_rows(block_in * moved[own])
    if first:
        out_ref[0] = jnp.where(mask, hgrad, 0.0)[own]
    else:
        out_ref[0] = hgrad


def add_pair(keep, received):
    total = keep + received.astype(f32)
    sent = total[1:].astype(low)
    return total[0], [sent[h] for h in range(sent.shape[0])]


def scattered(keep, send):
    own, sent = add_pair(keep, swap(send, "dp", 1))
    for h, piece in enumerate(sent):
        own = own + swap(piece, "dp", 2 * (h + 1)).astype(f32)
    return own


def over_seq(part):
    count = lax.axis_size("seq")
    cut = part.astype(low).reshape((count, part.shape[0] // count) + part.shape[1:])
    cut = by_owner(cut, "seq")
    total = cut[0].astype(f32)
    for d in range(1, count):
        total = total + swap(cut[d], "seq", d).astype(f32)
    total = total.astype(low)
    whole = by_owner([total] + [swap(total, "seq", d) for d in range(1, count)], "seq")
    return whole.reshape(part.shape).astype(f32)


def summed_everywhere(x):
    for axis in ("dp", "seq"):
        bit = 1
        while bit < lax.axis_size(axis):
            x = x + swap(x, axis, bit)
            bit *= 2
    return x


def per_device(
    features,
    lengths,
    dw_weight,
    block_gains,
    block_biases,
    up_weight,
    up_bias,
    down_weight,
    head_gain,
    head_shift,
    head_weight,
    head_bias,
    audio_grad,
):
    count = lax.axis_size("dp")
    pairs = count // 2
    micro = features.shape[0]
    rows = features.shape[2]
    width = features.shape[3]
    units = up_weight.shape[2]
    ext = rows + 2 * HALO
    seq_count = lax.axis_size("seq")
    seq_rows = rows * seq_count
    features = features[:, 0]
    audio_grad = audio_grad[:, 0]
    up_pairs = [(i, i + 1) for i in range(seq_count - 1)]
    down_pairs = [(i + 1, i) for i in range(seq_count - 1)]
    grad_low = audio_grad.astype(low)
    last = jnp.concatenate([features[:, rows - HALO :], grad_low[:, rows - HALO :]], axis=2)
    first = jnp.concatenate([features[:, :HALO], grad_low[:, :HALO]], axis=2)
    before = lax.ppermute(last, "seq", up_pairs)
    after = lax.ppermute(first, "seq", down_pairs)

    own = width // count
    gain_high = head_gain.astype(low)
    shift_high = head_shift.astype(low)
    small = jnp.concatenate(
        [
            dw_weight.reshape(-1, own),
            block_gains.reshape(-1, own),
            block_biases.reshape(-1, own),
            gain_high[None],
            (head_gain - gain_high.astype(f32)).astype(low)[None],
            shift_high[None],
            (head_shift - shift_high.astype(f32)).astype(low)[None],
            up_bias.reshape(-1, own),
        ]
    )
    even, odd = gathered(small)
    small = by_owner(jnp.stack([even, odd], axis=1).reshape((count,) + small.shape), "dp")
    split = small.shape[1] - BLOCKS * (units // width)
    wide = jnp.swapaxes(small[:, :split], 0, 1).reshape(split, width).astype(f32)
    up_bias_all = jnp.swapaxes(small[:, split:].reshape(count, BLOCKS, units // count), 0, 1)
    up_bias_all = up_bias_all.reshape(BLOCKS, 1, units).astype(f32)
    zero_row = jnp.zeros((1, width), f32)
    taps = [jnp.concatenate([wide[KERNEL * b : KERNEL * (b + 1)], zero_row]) for b in range(BLOCKS)]
    vecs = [
        jnp.concatenate([wide[14 + 2 * b : 16 + 2 * b], wide[18 + 3 * b : 21 + 3 * b], zero_row, zero_row, zero_row])
        for b in range(BLOCKS)
    ]
    head_vec = jnp.concatenate([wide[24:25] + wide[25:26], wide[26:27] + wide[27:28]] + [zero_row] * 6)

    def reordered(x, kind):
        return jnp.concatenate(
            [
                x[..., : BINS - 1],
                x[..., BINS : 2 * BINS - 1],
                x[..., BINS - 1 : BINS],
                x[..., 2 * BINS - 1 :],
                jnp.zeros(x.shape[:-1] + (EXTRA - 2,), kind),
            ],
            axis=-1,
        )

    head_low = reordered(head_weight.astype(low), low)
    head_bias_all = reordered(head_bias, f32)[None]
    ups = [None] * BLOCKS
    downs = [None] * BLOCKS
    for b in range(BLOCKS):
        ups[b] = gathered(up_weight[b])
        downs[b] = gathered(down_weight[b])
    head_pieces = gathered(head_low)

    row_ids = lax.axis_index("seq") * rows - HALO + jnp.arange(ext, dtype=jnp.int32)
    squared = jnp.asarray((window_values() ** 2).reshape(4, HOP), f32)
    envelope = jnp.zeros((ext, HOP), f32)
    for q in range(4):
        source = row_ids + 2 - q
        envelope = envelope + ((source >= 0) & (source < seq_rows)).astype(f32)[:, None] * squared[q]
    recip = jnp.where(((row_ids >= 0) & (row_ids < seq_rows))[:, None], 1.0 / envelope, 0.0)
    tables = jnp.asarray(head_tables())
    scal = jnp.concatenate(
        [
            jnp.stack([lax.axis_index("seq") * rows - HALO, jnp.int32(seq_rows), lax.axis_index("dp")]).astype(jnp.int32),
            lengths[:, 0],
        ]
    )

    extended = jnp.concatenate([before[..., :width], features, after[..., :width]], axis=1)
    grad_rows = jnp.concatenate([before[..., width:].astype(f32), audio_grad, after[..., width:].astype(f32)], axis=1)

    def shape(columns):
        return (micro, ext, columns)

    def dma(size=count):
        return pltpu.SemaphoreType.DMA((size,))

    run = functools.partial(call, grid=micro, scal=scal)
    cells = micro * ext
    (table_grad,) = run(
        functools.partial(dft_kernel, ext),
        ins=[(grad_rows, "rows"), (recip, "all"), (tables, "all")],
        outs=[(shape(NFFT), low, "rows")],
        scratch=[],
        flops=2 * cells * NFFT * NFFT,
        name="dft",
    )
    normed, unit, inv_std = run(
        functools.partial(conv_kernel, ext),
        ins=[(extended, "rows"), (taps[0], "all"), (vecs[0], "all")],
        outs=[(shape(width), low, "rows"), (shape(width), low, "rows"), (shape(1), f32, "rows")],
        scratch=[],
        flops=20 * cells * width,
        name="conv",
    )
    mm = 2 * cells * width * units
    saved = []
    source = extended
    for b in range(BLOCKS):
        act, slope = run(
            functools.partial(up_kernel, 256),
            ins=[(normed, "rows"), (up_bias_all[b], "all"), (ups[b][0], "any"), (ups[b][1], "any")],
            outs=[(shape(units), low, "rows"), (shape(units), low, "rows")],
            scratch=[pltpu.VMEM((width, units), low), dma()],
            flops=mm,
            name=f"up{b}",
        )
        final = b == BLOCKS - 1
        after_conv = [] if final else [(shape(width), low, "rows"), (shape(width), low, "rows"), (shape(1), f32, "rows")]
        results = run(
            functools.partial(down_kernel, ext, b == 0, final),
            ins=[
                (act, "rows"),
                (source, "rows"),
                (vecs[b], "all"),
                (taps[min(b + 1, BLOCKS - 1)], "all"),
                (vecs[min(b + 1, BLOCKS - 1)], "all"),
                (downs[b][0], "any"),
                (downs[b][1], "any"),
            ],
            outs=[(shape(width), f32, "rows"), (shape(width), low, "rows")] + after_conv,
            scratch=[pltpu.VMEM((units, width), low), dma()],
            flops=mm,
            name=f"down{b}",
        )
        saved.append((source, normed, unit, inv_std, act, slope, results[1]))
        source = results[0]
        if not final:
            normed, unit, inv_std = results[2:]

    columns = 2 * HALF + EXTRA
    audio, incoming, head_keep, head_send, head_small, bias_grad = run(
        functools.partial(head_kernel, ext, rows),
        ins=[
            (source, "rows"),
            (table_grad, "rows"),
            (recip, "all"),
            (tables, "all"),
            (head_vec, "all"),
            (head_bias_all, "all"),
            (head_pieces[0], "any"),
            (head_pieces[1], "any"),
        ],
        outs=[
            ((micro, rows, HOP), f32, "rows"),
            (shape(width), f32, "rows"),
            ((pairs, own, columns), f32, "all"),
            ((pairs, own, columns), low, "all"),
            ((8, width), f32, "all"),
            ((1, columns), f32, "all"),
        ],
        scratch=[pltpu.VMEM((width, columns), low), pltpu.VMEM((width, columns), f32), dma()],
        flops=2 * cells * (3 * width * columns + NFFT * NFFT),
        name="head",
    )
    head_part = scattered(head_keep, head_send)
    smalls = [None] * BLOCKS
    up_parts = [None] * BLOCKS
    down_parts = [None] * BLOCKS
    for b in reversed(range(BLOCKS)):
        block_source, normed, unit, inv_std, act, slope, branch = saved[b]
        pre_grad, keep, send, small_down, small_bias = run(
            functools.partial(back_down_kernel, rows, 512),
            ins=[
                (incoming, "rows"),
                (branch, "rows"),
                (act, "rows"),
                (slope, "rows"),
                (vecs[b], "all"),
                (downs[b][0], "any"),
                (downs[b][1], "any"),
            ],
            outs=[
                (shape(units), low, "rows"),
                ((pairs, units // count, width), f32, "all"),
                ((pairs, units // count, width), low, "all"),
                ((8, width), f32, "all"),
                ((1, units), f32, "all"),
            ],
            scratch=[pltpu.VMEM((units, width), low), pltpu.VMEM((units, width), f32), dma()],
            flops=2 * mm,
            name=f"back_down{b}",
        )
        down_parts[b] = scattered(keep, send)
        keep, send = run(
            functools.partial(up_grad_kernel, rows),
            ins=[(normed, "rows"), (pre_grad, "rows")],
            outs=[((pairs, own, units), f32, "all"), ((pairs, own, units), low, "all")],
            scratch=[pltpu.VMEM((width, units), f32)],
            flops=mm,
            name=f"up_grad{b}",
        )
        up_parts[b] = scattered(keep, send)
        kind = (micro, rows, width) if b == 0 else shape(width)
        incoming, small_conv = run(
            functools.partial(back_up_kernel, ext, rows, b == 0),
            ins=[
                (pre_grad, "rows"),
                (unit, "rows"),
                (inv_std, "rows"),
                (block_source, "rows"),
                (incoming, "rows"),
                (vecs[b], "all"),
                (taps[b], "all"),
                (ups[b][0], "any"),
                (ups[b][1], "any"),
            ],
            outs=[(kind, f32, "rows"), ((16, width), f32, "all")],
            scratch=[pltpu.VMEM((width, units), low), dma()],
            flops=mm,
            name=f"back_up{b}",
        )
        smalls[b] = (small_down, small_bias, small_conv)

    tap_rows = [smalls[b][2][:KERNEL] for b in range(BLOCKS)]
    gain_rows = [r for b in range(BLOCKS) for r in (smalls[b][2][8:9], smalls[b][0][0:1])]
    bias_rows = [r for b in range(BLOCKS) for r in (smalls[b][2][7:8], smalls[b][2][9:10], smalls[b][0][1:2])]
    small_grads = jnp.concatenate(
        [
            jnp.concatenate(tap_rows + gain_rows + bias_rows + [head_small[0:2]])
            .reshape(-1, count, own)
            .swapaxes(0, 1)
            .reshape(count, -1),
            jnp.concatenate([smalls[b][1] for b in range(BLOCKS)])
            .reshape(BLOCKS, count, -1)
            .swapaxes(0, 1)
            .reshape(count, -1),
        ],
        axis=1,
    )
    small_all = summed_everywhere(small_grads)
    mine = lax.dynamic_index_in_dim(small_all, lax.axis_index("dp"), 0, keepdims=False)
    bias_grad = summed_everywhere(bias_grad)[0]
    entries = mine[: 26 * own].reshape(26, own)
    head_part = over_seq(head_part)

    def restored(x):
        return jnp.concatenate(
            [
                x[..., :HALF],
                x[..., 2 * HALF : 2 * HALF + 1],
                x[..., HALF : 2 * HALF],
                x[..., 2 * HALF + 1 : 2 * HALF + 2],
            ],
            axis=-1,
        )

    return (
        audio[:, None],
        incoming[:, None],
        entries[:14].reshape(BLOCKS, KERNEL, own),
        entries[14:18].reshape(BLOCKS, 2, own),
        entries[18:24].reshape(BLOCKS, 3, own),
        jnp.stack([over_seq(up_parts[b]) for b in range(BLOCKS)]),
        mine[26 * own :].reshape(BLOCKS, -1),
        jnp.stack([over_seq(down_parts[b]) for b in range(BLOCKS)]),
        entries[24],
        entries[25],
        restored(head_part),
        restored(bias_grad),
    )


def solution(mesh):
    return jax.shard_map(
        per_device,
        mesh=mesh,
        in_specs=(
            P(None, "dp", "seq", None),
            P(None, "dp"),
            P(None, None, "dp"),
            P(None, None, "dp"),
            P(None, None, "dp"),
            P(None, "dp", None),
            P(None, "dp"),
            P(None, "dp", None),
            P("dp"),
            P("dp"),
            P("dp", None),
            P(),
            P(None, "dp", "seq", None),
        ),
        out_specs=(
            P(None, "dp", "seq", None),
            P(None, "dp", "seq", None),
            P(None, None, "dp"),
            P(None, None, "dp"),
            P(None, None, "dp"),
            P(None, "dp", None),
            P(None, "dp"),
            P(None, "dp", None),
            P("dp"),
            P("dp"),
            P("dp", None),
            P(),
        ),
        check_vma=False,
    )
```

```python
import functools
import math

import jax
import jax.numpy as jnp
import numpy as np
from jax import lax
from jax.experimental import pallas as pl
from jax.experimental.pallas import tpu as pltpu
from jax.sharding import PartitionSpec as P

NFFT = 1024
HOP = 256
BINS = 513
HALF = 512
EXTRA = 128
KERNEL = 7
BLOCKS = 2
HALO = 16
SMALL = 32
norm_eps = 1e-06
f32 = jnp.float32
low = jnp.bfloat16
rows_dims = (((0,), (0,)), ((), ()))
cols_dims = (((1,), (1,)), ((), ()))
MiB = 2**20
GELU = (0.7978202661111929, 0.03654664812915587, -0.00019444764679970054, -1.3688682486738934e-05)
SIN = (6.283184921107194, -41.34159015596926, 81.59997289449204, -76.61480381354174, 41.34439732745281, -12.473668162531846)
COS = (0.9999992215705861, -19.738982516102407, 64.92872660899411, -85.27239689575316, 58.79403819232432, -21.076781286284348)


def window_values():
    return 0.5 - 0.5 * np.cos(np.arange(NFFT) * (2.0 * math.pi / NFFT))


def head_tables():
    row = np.arange(NFFT)
    frequency = np.where(row < HALF, row, np.where(row == HALF, HALF, row - HALF))
    angles = (frequency[:, None] * np.arange(NFFT)[None, :] % NFFT) * (2.0 * math.pi / NFFT)
    weight = np.where((row == 0) | (row == HALF), 1.0, 2.0)[:, None] / NFFT
    values = np.where((row <= HALF)[:, None], np.cos(angles), -np.sin(angles)) * weight
    return (values * window_values()[None, :]).astype(jnp.bfloat16)


def swap(x, axis, d):
    return lax.ppermute(x, axis, [(i, i ^ d) for i in range(lax.axis_size(axis))])


def poly(z, coefficients):
    p = coefficients[-1]
    for c in coefficients[-2::-1]:
        p = p * z + c
    return p


def gelu_parts(x):
    u = jnp.clip(x, -5.2, 5.2)
    z = u * u
    p = poly(z, [jnp.asarray(c, x.dtype) for c in GELU])
    half = jnp.asarray(0.5, x.dtype)
    cumulative = half * jnp.tanh(u * p) + half
    density = jnp.exp2(z * jnp.asarray(-0.5 * math.log2(math.e), x.dtype))
    return x * cumulative, cumulative + (x * jnp.asarray(1.0 / math.sqrt(2.0 * math.pi), x.dtype)) * density


def norm_parts(values):
    centred = values - jnp.mean(values, axis=1, keepdims=True)
    inv_std = lax.rsqrt(jnp.mean(centred * centred, axis=1, keepdims=True) + norm_eps)
    return centred * inv_std, inv_std


def norm_back(normed_grad, unit, inv_std, gain):
    unit_grad = normed_grad * gain
    inner = jnp.mean(unit_grad * unit, axis=1, keepdims=True)
    return inv_std * (unit_grad - jnp.mean(unit_grad, axis=1, keepdims=True) - unit * inner)


def total_rows(x):
    return jnp.sum(x, axis=0, keepdims=True)


def row(ref, i):
    return ref[i : i + 1]


def turns(x):
    r = x * (1.0 / (2.0 * math.pi))
    r = r - jnp.floor(r + 0.5)
    z = r * r
    return poly(z, COS), r * poly(z, SIN)


class Frames:
    def __init__(self, rows, lengths_ref):
        self.rows = rows
        self.ext = rows + 2 * HALO
        self.own = slice(HALO, HALO + rows)
        self.start = lax.axis_index("seq") * rows - HALO
        self.total = rows * lax.axis_size("seq")
        self.length = lengths_ref[pl.program_id(0), 0]
        self.tiles = [(0, HALO)] + [(r, 32) for r in range(HALO, HALO + rows, 32)] + [(HALO + rows, HALO)]
        self.half = self.ext // 2

    def at(self, r=0, n=None):
        return lax.broadcasted_iota(jnp.int32, (n or self.ext, 1), 0) + (self.start + r)

    def inside(self, r=0, n=None):
        t = self.at(r, n)
        return (t >= 0) & (t < self.total)

    def mask(self, r=0, n=None):
        t = self.at(r, n)
        return (t >= 0) & (t < self.total) & (t < self.length)

    def owns(self, r):
        return HALO <= r < HALO + self.rows

    def parts(self):
        return [(r0, range(r0, r0 + self.half, 16)) for r0 in (0, self.half)]


def feature_tile(frames, before_ref, features_ref, after_ref, r, n):
    width = features_ref.shape[2]
    if r < HALO:
        tile = before_ref[0, r : r + n, :width]
    elif r < HALO + frames.rows:
        tile = features_ref[0, r - HALO : r - HALO + n]
    else:
        tile = after_ref[0, r - HALO - frames.rows : r - HALO - frames.rows + n, :width]
    return jnp.where(frames.mask(r, n), tile.astype(f32), 0.0)


def fold(x):
    total = x[0:8]
    for r in range(8, x.shape[0], 8):
        total = total + x[r : r + 8]
    return total


def add_to(ref, i, x):
    ref[8 * i : 8 * i + 8] += fold(x)


def assemble(even_ref, odd_ref, size, whole_ref, sems):
    me = lax.axis_index("dp")
    copies = []
    for h in range(even_ref.shape[0]):
        for c, ref in enumerate((even_ref, odd_ref)):
            at = pl.multiple_of((me ^ (2 * h + c)) * size, size)
            copies.append(
                pltpu.make_async_copy(ref.at[h, pl.ds(0, size)], whole_ref.at[pl.ds(at, size)], sems.at[2 * h + c])
            )
    return copies


def run_copies(copies):
    for copy in copies:
        copy.start()
    for copy in copies:
        copy.wait()


def skipping(kernel, start, count):
    def inner(*refs):
        return kernel(*refs[:start], *refs[start + count :])

    return inner if count else kernel


def in_hbm(x):
    return pltpu.with_memory_space_constraint(x, pltpu.HBM)


def cost(us):
    return pl.CostEstimate(flops=1000 + int(us * 1e9), bytes_accessed=1000, transcendentals=0)


def call(kernel, grid, lengths, ins, outs, scratch, name, after=(), limit=48, us=0):
    def spec(shape, kind):
        if isinstance(kind, pl.BlockSpec):
            return kind
        if kind == "any":
            return pl.BlockSpec(memory_space=pl.ANY)
        if kind == "rows":
            return pl.BlockSpec((1,) + tuple(shape[1:]), lambda i, s: (i,) + (0,) * (len(shape) - 1))
        return pl.BlockSpec(tuple(shape), lambda i, s: (0,) * len(shape))

    kernel = skipping(kernel, 1 + len(ins), len(after))
    ins = ins + [(a, "any") for a in after]
    return pl.pallas_call(
        kernel,
        out_shape=[(pltpu.HBM if kind == "rows" else jax.ShapeDtypeStruct)(tuple(s), d) for s, d, kind in outs],
        grid_spec=pltpu.PrefetchScalarGridSpec(
            num_scalar_prefetch=1,
            grid=(grid,),
            in_specs=[spec(a.shape, kind) for a, kind in ins],
            out_specs=[spec(s, kind) for s, _, kind in outs],
            scratch_shapes=scratch,
        ),
        compiler_params=pltpu.CompilerParams(vmem_limit_bytes=limit * MiB, dimension_semantics=("arbitrary",)),
        cost_estimate=cost(us),
        name=name,
    )(lengths, *[in_hbm(a) if kind == "rows" and a.shape[1] != HALO else a for a, kind in ins])


def simple_call(kernel, ins, outs, name, scratch=(), after=(), limit=16, us=0):
    whole = pl.BlockSpec(memory_space=pltpu.VMEM)
    return pl.pallas_call(
        skipping(kernel, len(ins), len(after)),
        out_shape=[jax.ShapeDtypeStruct(tuple(s), d) for s, d in outs],
        in_specs=[whole] * len(ins) + [pl.BlockSpec(memory_space=pl.ANY)] * len(after),
        out_specs=[whole] * len(outs),
        scratch_shapes=list(scratch),
        compiler_params=pltpu.CompilerParams(vmem_limit_bytes=limit * MiB),
        cost_estimate=cost(us),
        name=name,
    )(*ins, *after)


def head_columns(x):
    lane = lax.broadcasted_iota(jnp.int32, (x.shape[0], EXTRA), 1)
    tail = jnp.where(lane == 0, x[:, BINS - 1 : BINS], jnp.where(lane == 1, x[:, 2 * BINS - 1 :], 0.0))
    return x[:, : BINS - 1], x[:, BINS : 2 * BINS - 1], tail


def pack_kernel(
    first_ref, last_ref, gfirst_ref, glast_ref, dw_ref, gains_ref, biases_ref, upb_ref, hgain_ref, hshift_ref,
    head_ref, up_ref, down_ref, first_out, last_out, up0_out, rest_out,
):
    width = first_ref.shape[2]
    first_out[:, :, :width] = first_ref[...]
    first_out[:, :, width:] = gfirst_ref[...].astype(low)
    last_out[:, :, :width] = last_ref[...]
    last_out[:, :, width:] = glast_ref[...].astype(low)
    own = up_ref.shape[1]
    up0_out[0:own] = up_ref[0]
    up0_out[own:] = jnp.zeros((16, up_ref.shape[2]), low)

    def stack(parts):
        parts = [p.astype(f32) for p in parts]
        filled = sum(p.shape[0] for p in parts)
        return jnp.concatenate(parts + [jnp.zeros((16 - filled, parts[0].shape[1]), f32)], axis=0).astype(low)

    def halves(x):
        high = x.astype(low).astype(f32)
        return [high, x - high]

    up0_out[own:, 0:own] = stack([dw_ref[:, 0, :], dw_ref[:, 1, :]])
    up0_out[own:, 128 : 128 + own] = stack(
        [gains_ref[0], gains_ref[1], biases_ref[:, 0, :], biases_ref[:, 1, :]] + halves(hgain_ref[...]) + halves(hshift_ref[...])
    )
    up0_out[own:, 256 : 256 + upb_ref.shape[1]] = stack([upb_ref[...]])
    size = down_ref.shape[1]
    base = up_ref.shape[2] // HALF * own
    for g in range(0, up_ref.shape[2], HALF):
        rest_out[g // HALF * own : (g // HALF + 1) * own] = up_ref[1, :, g : g + HALF]
    rest_out[base : base + size] = down_ref[1]
    size = base + size

    magnitude, phase, tail = head_columns(head_ref[...])
    rest_out[size : size + own] = magnitude.astype(low)
    rest_out[size + own : size + 2 * own] = phase.astype(low)
    rest_out[size + 2 * own :] = jnp.zeros((own, HALF), low)
    rest_out[size + 2 * own :, :EXTRA] = tail.astype(low)


def dft_kernel(rows, lengths, before_ref, grad_ref, after_ref, squared_ref, table_ref, out_ref, recip_ref):
    frames = Frames(rows, lengths)
    width = before_ref.shape[2] - HOP

    @pl.when(pl.program_id(0) == 0)
    def _():
        envelope = jnp.zeros((frames.ext, HOP), f32)
        for q in range(4):
            source = frames.at() + (2 - q)
            valid = (source >= 0) & (source < frames.total)
            envelope = envelope + jnp.where(valid, row(squared_ref, q), 0.0)
        recip_ref[...] = jnp.where(frames.inside(), 1.0 / envelope, 0.0)

    whole = jnp.concatenate(
        [before_ref[0, :, width:].astype(f32), grad_ref[0], after_ref[0, :, width:].astype(f32)], axis=0
    )
    own = jnp.where(frames.mask(), whole * recip_ref[...], 0.0)
    parts = [own if q == 2 else pltpu.roll(own, (2 - q) % frames.ext, 0) for q in range(4)]
    framed = jnp.where(frames.inside(), jnp.concatenate(parts, axis=1), 0.0).astype(low)
    out_ref[0] = lax.dot_general(framed, table_ref[...], cols_dims, preferred_element_type=f32).astype(low)


def put_padded(pad_ref, frames, tile_of):
    zeros = jnp.zeros((8, pad_ref.shape[1]), f32)
    pad_ref[0:8] = zeros
    pad_ref[frames.ext + 8 :] = zeros
    for r, n in frames.tiles:
        pad_ref[8 + r : 8 + r + n] = tile_of(r, n)


def conv_tile(pad_ref, r, n, taps_ref, base, bias):
    window = pad_ref[r : r + n + 16]
    conv = bias + row(taps_ref, base + 3) * window[8 : 8 + n]
    for k in range(KERNEL):
        if k != 3:
            conv = conv + row(taps_ref, base + k) * pltpu.roll(window, (3 - k) % (n + 16), 0)[8 : 8 + n]
    return conv


def conv_norm(frames, pad_ref, taps_ref, base, vec_ref, b, unit_at, inv_at, normed_at):
    for r, n in frames.tiles:
        unit, inv_std = norm_parts(conv_tile(pad_ref, r, n, taps_ref, base, bias_row(vec_ref, b, 0)))
        unit_at[r : r + n] = unit.astype(unit_at.dtype)
        inv_at[r : r + n] = inv_std
        normed_at[r : r + n] = (unit * gain_row(vec_ref, b, 0) + bias_row(vec_ref, b, 1)).astype(low)


def gain_row(ref, b, i):
    return row(ref, 2 * b + i)


def bias_row(ref, b, i):
    return row(ref, 4 + 3 * b + i)


def conv_kernel(
    rows, own, units, lengths, before_ref, features_ref, after_ref, hbias_ref, even_ref, odd_ref,
    normed_ref, unit_ref, inv_ref, taps_ref, vec_ref, upb_ref, bias_ref, small_ref, pad_ref, sems,
):
    @pl.when(pl.program_id(0) == 0)
    def _():
        me = lax.axis_index("dp")
        count = 2 * even_ref.shape[0]
        copies = []
        for d in range(count):
            ref = odd_ref if d % 2 else even_ref
            copies.append(
                pltpu.make_async_copy(ref.at[d // 2, pl.ds(own, 16), pl.ds(0, small_ref.shape[2])], small_ref.at[d], sems.at[d])
            )
        run_copies(copies)

        def spread(lanes, size, out_ref):
            total = jnp.zeros(out_ref.shape, f32)
            at = lax.broadcasted_iota(jnp.int32, (size, out_ref.shape[1]), 0)
            to = lax.broadcasted_iota(jnp.int32, (size, out_ref.shape[1]), 1)
            for d in range(count):
                place = jnp.where(to == at + (me ^ d) * size, 1.0, 0.0).astype(low)
                total = total + jnp.dot(small_ref[d, :, lanes : lanes + size], place, preferred_element_type=f32)
            out_ref[...] = total

        spread(0, own, taps_ref)
        spread(128, own, vec_ref)
        spread(256, units // count, upb_ref)
        magnitude, phase, tail = head_columns(hbias_ref[...])
        bias_ref[:, :HALF] = magnitude
        bias_ref[:, HALF : 2 * HALF] = phase
        bias_ref[:, 2 * HALF :] = tail

    frames = Frames(rows, lengths)
    put_padded(pad_ref, frames, functools.partial(feature_tile, frames, before_ref, features_ref, after_ref))
    conv_norm(frames, pad_ref, taps_ref, 0, vec_ref, 0, unit_ref.at[0], inv_ref.at[0], normed_ref.at[0])


def up_gelu(frames, normed_at, weight_ref, bias, act_at, slope_at, chunk=256):
    for r0, _ in frames.parts():
        normed = normed_at[r0 : r0 + frames.half]
        for c in range(0, weight_ref.shape[1], chunk):
            pre = jnp.dot(normed, weight_ref[:, c : c + chunk], preferred_element_type=f32) + bias[:, c : c + chunk]
            act, slope = gelu_parts(pre.astype(low))
            act_at[r0 : r0 + frames.half, c : c + chunk] = act
            slope_at[r0 : r0 + frames.half, c : c + chunk] = slope


def forward_kernel(
    rows, own, size, lengths, before_ref, features_ref, after_ref, normed_ref, vec_ref, upb_ref,
    ueven_ref, uodd_ref, deven_ref, dodd_ref, hidden_ref, act_ref, slope_ref, branch_ref, up_ref, down_ref, sems, sems2,
):
    @pl.when(pl.program_id(0) == 0)
    def _():
        run_copies(assemble(ueven_ref, uodd_ref, own, up_ref, sems) + assemble(deven_ref, dodd_ref, size, down_ref, sems2))

    frames = Frames(rows, lengths)
    act_at = act_ref.at[0]
    up_gelu(frames, normed_ref.at[0], up_ref, row(upb_ref, 0), act_at, slope_ref.at[0])
    for r0, tiles in frames.parts():
        product = jnp.dot(act_at[r0 : r0 + frames.half], down_ref[...], preferred_element_type=f32)
        for r in tiles:
            branch = product[r - r0 : r - r0 + 16] + bias_row(vec_ref, 0, 2)
            branch_ref[0, r : r + 16] = branch.astype(low)
            h = feature_tile(frames, before_ref, features_ref, after_ref, r, 16)
            hidden_ref[0, r : r + 16] = h + gain_row(vec_ref, 0, 1) * branch


def split_rows(total_at, size, keep_at, send_at, pieces):
    me = lax.axis_index("dp")
    for h in range(pieces):
        at = pl.multiple_of((me ^ (2 * h)) * size, size)
        keep_at(h, total_at(pl.ds(at, size)).astype(low))
        at = pl.multiple_of((me ^ (2 * h + 1)) * size, size)
        send_at(h, total_at(pl.ds(at, size)).astype(low))


def give(ref, base):
    def put(h, value):
        ref[h, base : base + value.shape[0], : value.shape[1]] = value

    return put


def split_columns(total_ref, base, size, keep_ref, send_ref):
    for g in range(0, total_ref.shape[1], HALF):
        stop = min(g + HALF, total_ref.shape[1])
        at = base + g // HALF * size
        split_rows(lambda r: total_ref[r, g:stop], size, give(keep_ref, at), give(send_ref, at), keep_ref.shape[0])


def branch_tile(frames, r, hgrad, branch, gain, bgrad_at, sums_ref, at):
    bgrad = (gain * hgrad).astype(low)
    bgrad_at[r : r + 16] = bgrad
    if frames.owns(r):
        add_to(sums_ref, at, hgrad * branch.astype(f32))
        add_to(sums_ref, at + 1, bgrad.astype(f32))


def back_down(frames, bgrad_at, act_at, slope_at, weight_ref, total_ref, pgrad_at, bsums_ref, chunk=512):
    own = frames.own
    for c in range(0, weight_ref.shape[0], chunk):
        part = slice(c, c + chunk)
        for r0, tiles in frames.parts():
            act_grad = lax.dot_general(bgrad_at[r0 : r0 + frames.half], weight_ref[part], cols_dims, preferred_element_type=f32)
            for r in tiles:
                grad = (act_grad[r - r0 : r - r0 + 16] * slope_at[r : r + 16, part].astype(f32)).astype(low)
                pgrad_at[r : r + 16, part] = grad
                if frames.owns(r):
                    bsums_ref[:, part] += fold(grad.astype(f32))
        total_ref[part] += lax.dot_general(act_at[own, part], bgrad_at[own], rows_dims, preferred_element_type=f32)


def back_up_norm(frames, pgrad_at, unit_at, inv_at, gain, weight_ref, pad_ref, sums_ref):
    zeros = jnp.zeros((8, pad_ref.shape[1]), f32)
    pad_ref[0:8] = zeros
    pad_ref[frames.ext + 8 :] = zeros
    for r0, tiles in frames.parts():
        product = lax.dot_general(pgrad_at[r0 : r0 + frames.half], weight_ref[...], cols_dims, preferred_element_type=f32)
        for r in tiles:
            normed_grad = product[r - r0 : r - r0 + 16]
            unit = unit_at[r : r + 16].astype(f32)
            conv_grad = norm_back(normed_grad, unit, inv_at[r : r + 16], gain)
            if frames.owns(r):
                conv_grad = conv_grad.astype(low).astype(f32)
                add_to(sums_ref, 7, conv_grad)
                add_to(sums_ref, 8, normed_grad * unit)
                add_to(sums_ref, 9, normed_grad)
            else:
                conv_grad = jnp.where(frames.inside(r, 16), conv_grad, 0.0).astype(low).astype(f32)
            pad_ref[8 + r : 8 + r + 16] = conv_grad


def conv_back_tile(frames, r, n, pad_ref, block_in_of, hgrad, taps_ref, base, sums_ref):
    window = pad_ref[r : r + n + 16]
    owns = frames.owns(r)
    block_in = block_in_of(r, n) if owns else None
    for k in range(KERNEL):
        moved = (window if k == 3 else pltpu.roll(window, (k - 3) % (n + 16), 0))[8 : 8 + n]
        hgrad = hgrad + row(taps_ref, base + k) * moved
        if owns:
            add_to(sums_ref, k, block_in * moved)
    return hgrad


def close_sums(sums_ref, small_ref):
    for i in range(sums_ref.shape[0] // 8):
        small_ref[i : i + 1] = total_rows(sums_ref[8 * i : 8 * i + 8])


def middle_kernel(
    rows, own, size, lengths, h_ref, tgrad_ref, recip_ref, taps_ref, vec_ref, upb_ref, bias_ref,
    table_hbm, rest_ref,
    audio_ref, hgrad_ref, keep_ref, send_ref, small_ref, sbias_ref,
    table_ref, up_ref, down_ref, head_ref, head_total, up_total, down_total, act_ref, slope_ref,
    pad_ref, cpad_ref, frame_ref, unit1_ref, unit2_ref, inv1_ref, inv2_ref, normed1_ref, normed2_ref, turned_ref,
    branch_ref, bgrad_ref, spectrum_ref, lgrad_ref, sums_ref, bsums_ref, hsums_ref, sems,
):
    step = pl.program_id(0)

    @pl.when(step == 0)
    def _():
        copies = []
        groups = up_ref.shape[1] // HALF
        places = [(g * own, own, up_ref, g * HALF, HALF) for g in range(groups)]
        places.append((groups * own, size, down_ref, 0, HALF))
        base = groups * own + size
        places += [(base + g * own, own, head_ref, g * HALF, lanes) for g, lanes in enumerate((HALF, HALF, EXTRA))]
        for j in range(rest_ref.shape[0]):
            for i, (at, many, ref, lane, lanes) in enumerate(places):
                copies.append(
                    pltpu.make_async_copy(
                        rest_ref.at[j, pl.ds(at, many), pl.ds(0, lanes)],
                        ref.at[pl.ds(j * many, many), pl.ds(lane, lanes)],
                        sems.at[j, i],
                    )
                )
        copies.append(pltpu.make_async_copy(table_hbm, table_ref, sems.at[0, len(places)]))
        for copy in copies:
            copy.start()
        for ref in (head_total, up_total, down_total, sums_ref, bsums_ref, hsums_ref):
            ref[...] = jnp.zeros_like(ref)
        for copy in copies:
            copy.wait()

    frames = Frames(rows, lengths)
    mine, half, ext = frames.own, frames.half, frames.ext

    def block_in_tile(r, n):
        return jnp.where(frames.inside(r, n), h_ref[0, r : r + n], 0.0).astype(low).astype(f32)

    put_padded(pad_ref, frames, block_in_tile)
    conv_norm(frames, pad_ref, taps_ref, KERNEL, vec_ref, 1, unit1_ref, inv1_ref, normed1_ref)
    up_gelu(frames, normed1_ref, up_ref, row(upb_ref, 1), act_ref, slope_ref)

    head_gain = row(vec_ref, 10) + row(vec_ref, 11)
    head_shift = row(vec_ref, 12) + row(vec_ref, 13)
    for r0, tiles in frames.parts():
        product = jnp.dot(act_ref[r0 : r0 + half], down_ref[...], preferred_element_type=f32)
        for r in tiles:
            branch = product[r - r0 : r - r0 + 16] + bias_row(vec_ref, 1, 2)
            branch_ref[r : r + 16] = branch.astype(low)
            unit, inv_std = norm_parts(h_ref[0, r : r + 16] + gain_row(vec_ref, 1, 1) * branch)
            unit2_ref[r : r + 16] = unit
            inv2_ref[r : r + 16] = inv_std
            normed2_ref[r : r + 16] = (unit * head_gain + head_shift).astype(low)

    lane = lax.broadcasted_iota(jnp.int32, (16, EXTRA), 1)
    for r0, tiles in frames.parts():
        product = jnp.dot(normed2_ref[r0 : r0 + half], head_ref[...], preferred_element_type=f32)
        for r in tiles:
            logits = product[r - r0 : r - r0 + 16] + bias_ref[...]
            magnitude = jnp.exp(logits[:, :HALF])
            cos, sin = turns(logits[:, HALF : 2 * HALF])
            re = magnitude * cos
            im = magnitude * sin
            last = logits[:, 2 * HALF :]
            cos, sin = turns(pltpu.roll(last, EXTRA - 1, 1))
            top = jnp.exp(jnp.where(lane == 0, last, 0.0))
            top_re = top * cos
            top_im = top * sin
            spectrum_ref[r : r + 16, :HALF] = re.astype(low)
            spectrum_ref[r : r + 16, HALF : HALF + EXTRA] = jnp.where(lane == 0, top_re, im[:, :EXTRA]).astype(low)
            spectrum_ref[r : r + 16, HALF + EXTRA :] = im[:, EXTRA:].astype(low)
            tgrad = tgrad_ref[0, r : r + 16].astype(f32)
            re_grad = tgrad[:, :HALF]
            top_grad = tgrad[:, HALF : HALF + EXTRA]
            im_grad = jnp.concatenate([jnp.where(lane == 0, 0.0, top_grad), tgrad[:, HALF + EXTRA :]], axis=1)
            log_last = jnp.where(lane == 0, top_grad * top_re, 0.0)
            phase_last = jnp.where(lane == 1, pltpu.roll(top_grad * top_im, 1, 1), 0.0)
            grads = (re_grad * re + im_grad * im, im_grad * re - re_grad * im, log_last - phase_last)
            for g, grad in enumerate(grads):
                part = slice(g * HALF, g * HALF + grad.shape[1])
                lgrad_ref[r : r + 16, part] = grad.astype(low)
                if frames.owns(r):
                    hsums_ref[:, part] += fold(grad)

    for r0, tiles in frames.parts():
        product = jnp.dot(spectrum_ref[r0 : r0 + half], table_ref[...], preferred_element_type=f32)
        for r in tiles:
            framed = product[r - r0 : r - r0 + 16]
            if not frames.owns(r):
                framed = jnp.where(frames.inside(r, 16), framed, 0.0)
            frame_ref[8 + r : 8 + r + 16] = framed

    hgrad_at = hgrad_ref.at[0]
    for r0, tiles in frames.parts():
        product = lax.dot_general(lgrad_ref[r0 : r0 + half], head_ref[...], cols_dims, preferred_element_type=f32)
        for r in tiles:
            normed_grad = product[r - r0 : r - r0 + 16]
            unit = unit2_ref[r : r + 16]
            hgrad = norm_back(normed_grad, unit, inv2_ref[r : r + 16], head_gain)
            hgrad_at[r : r + 16] = hgrad
            if frames.owns(r):
                add_to(sums_ref, 12, normed_grad * unit)
                add_to(sums_ref, 13, normed_grad)
            branch_tile(frames, r, hgrad, branch_ref[r : r + 16], gain_row(vec_ref, 1, 1), bgrad_ref, sums_ref, 10)

    def audio_tile(r, n):
        audio = frame_ref[8 + r : 8 + r + n, 2 * HOP : 3 * HOP]
        for q in (0, 1, 3):
            window = frame_ref[r : r + n + 16, q * HOP : (q + 1) * HOP]
            audio = audio + pltpu.roll(window, (q - 2) % (n + 16), 0)[8 : 8 + n]
        audio_ref[0, r - HALO : r - HALO + n] = jnp.where(frames.mask(r, n), audio * recip_ref[r : r + n], 0.0)

    def beside(chunks, tiles, dot_of, put, work):
        each = -(-len(tiles) // len(chunks))
        for i, part in enumerate(chunks):
            product = dot_of(part)
            for r, n in tiles[i * each : (i + 1) * each]:
                work(r, n)
            put(part, product)

    own_tiles = [tile for tile in frames.tiles if frames.owns(tile[0])]
    turned_ref[...] = normed2_ref[mine].T

    def put_head(part, product):
        head_total[:, part] += product

    beside(
        [slice(c, c + 384) for c in range(0, head_total.shape[1], 384)],
        own_tiles,
        lambda part: jnp.dot(turned_ref[...], lgrad_ref[mine, part], preferred_element_type=f32),
        put_head,
        audio_tile,
    )

    back_down(frames, bgrad_ref, act_ref, slope_ref, down_ref, down_total, slope_ref, bsums_ref)
    back_up_norm(frames, slope_ref, unit1_ref, inv1_ref, gain_row(vec_ref, 1, 0), up_ref, cpad_ref, sums_ref)
    turned_ref[...] = normed1_ref[mine].T

    def put_up(part, product):
        up_total[:, part] += product

    def conv_back(r, n):
        hgrad_at[r : r + n] = conv_back_tile(
            frames, r, n, cpad_ref, lambda r, n: pad_ref[8 + r : 8 + r + n], hgrad_at[r : r + n], taps_ref, KERNEL, sums_ref
        )

    beside(
        [slice(c, c + 256) for c in range(0, up_total.shape[1], 256)],
        frames.tiles,
        lambda part: jnp.dot(turned_ref[...], slope_ref[mine, part], preferred_element_type=f32),
        put_up,
        conv_back,
    )

    @pl.when(step == pl.num_programs(0) - 1)
    def _():
        close_sums(sums_ref, small_ref)
        sbias_ref[...] = total_rows(bsums_ref[...])
        groups = up_ref.shape[1] // HALF * own
        split_columns(up_total, 0, own, keep_ref, send_ref)
        split_columns(down_total, groups, size, keep_ref, send_ref)
        base = groups + size
        bias = total_rows(hsums_ref[...])
        block = jnp.concatenate([bias[:, g : g + 384] for g in (0, 384, 768)] + [jnp.zeros((13, 384), f32)], axis=0)
        for h in range(keep_ref.shape[0]):
            for ref in (keep_ref, send_ref):
                ref[h, base + 2 * own :] = jnp.zeros((own, HALF), low)
                ref[h, base + 2 * own : base + 2 * own + 16, EXTRA:] = block.astype(low)
        split_columns(head_total, base, own, keep_ref, send_ref)


def back_down_kernel(
    rows, own, size, lengths, hgrad_ref, branch_ref, act_ref, slope_ref, normed_ref, vec_ref, even_ref, odd_ref,
    pgrad_ref, keep_ref, send_ref, small_ref, sbias_ref, weight_ref, down_total, up_total, bgrad_ref, sums_ref, bsums_ref, sems,
):
    step = pl.program_id(0)

    @pl.when(step == 0)
    def _():
        copies = assemble(even_ref, odd_ref, size, weight_ref, sems)
        for copy in copies:
            copy.start()
        for ref in (down_total, up_total, sums_ref, bsums_ref):
            ref[...] = jnp.zeros_like(ref)
        for copy in copies:
            copy.wait()

    frames = Frames(rows, lengths)
    mine = frames.own
    for r in range(0, frames.ext, 16):
        branch_tile(frames, r, hgrad_ref[0, r : r + 16], branch_ref[0, r : r + 16], gain_row(vec_ref, 0, 1), bgrad_ref, sums_ref, 0)
    back_down(frames, bgrad_ref, act_ref.at[0], slope_ref.at[0], weight_ref, down_total, pgrad_ref.at[0], bsums_ref)
    up_total[...] += lax.dot_general(normed_ref[0, mine], pgrad_ref[0, mine], rows_dims, preferred_element_type=f32)

    @pl.when(step == pl.num_programs(0) - 1)
    def _():
        close_sums(sums_ref, small_ref)
        sbias_ref[...] = total_rows(bsums_ref[...])
        split_columns(up_total, 0, own, keep_ref, send_ref)
        split_columns(down_total, up_total.shape[1] // HALF * own, size, keep_ref, send_ref)


def back_up_kernel(
    rows, own, lengths, pgrad_ref, unit_ref, inv_ref, features_ref, hgrad_ref, taps_ref, vec_ref, even_ref, odd_ref,
    out_ref, small_ref, weight_ref, pad_ref, sums_ref, sems,
):
    step = pl.program_id(0)

    @pl.when(step == 0)
    def _():
        sums_ref[...] = jnp.zeros_like(sums_ref)
        run_copies(assemble(even_ref, odd_ref, own, weight_ref, sems))

    frames = Frames(rows, lengths)
    back_up_norm(
        frames, pgrad_ref.at[0], unit_ref.at[0], inv_ref.at[0], gain_row(vec_ref, 0, 0), weight_ref, pad_ref, sums_ref
    )

    def block_in_tile(r, n):
        return jnp.where(frames.mask(r, n), features_ref[0, r - HALO : r - HALO + n].astype(f32), 0.0)

    for r, n in frames.tiles:
        if frames.owns(r):
            hgrad = conv_back_tile(frames, r, n, pad_ref, block_in_tile, hgrad_ref[0, r : r + n], taps_ref, 0, sums_ref)
            out_ref[0, r - HALO : r - HALO + n] = jnp.where(frames.mask(r, n), hgrad, 0.0)

    @pl.when(step == pl.num_programs(0) - 1)
    def _():
        close_sums(sums_ref, small_ref)


def small_kernel(conv0_ref, down0_ref, bias0_ref, mid_ref, bias1_ref, out_ref):
    width = out_ref.shape[1]
    groups = [r[:, g : g + width] for r in (bias0_ref, bias1_ref) for g in range(0, r.shape[1], width)]
    rows = [
        conv0_ref[0:7], mid_ref[0:7],
        conv0_ref[8:9], down0_ref[0:1], mid_ref[8:9], mid_ref[10:11],
        conv0_ref[7:8], conv0_ref[9:10], down0_ref[1:2], mid_ref[7:8], mid_ref[9:10], mid_ref[11:12],
        mid_ref[12:14],
    ] + groups
    filled = 26 + len(groups)
    rows = rows + [jnp.zeros((out_ref.shape[0] - filled, width), f32)] * (filled < out_ref.shape[0])
    out_ref[...] = jnp.concatenate(rows, axis=0).astype(low)


def gather_kernel(pieces, at, *refs):
    for h in range(pieces):
        refs[-1 if len(refs) == pieces + 1 else pieces + 1][h] = refs[h][...]
    if len(refs) > pieces + 1:
        refs[-1][...] = refs[pieces][at]


def final_kernel(
    own, size, parts, late_ref, *refs,
):
    part_refs = refs[:parts]
    up_ref, down_ref, head_ref, hbias_ref, dw_ref, gains_ref, biases_ref, upb_ref, hgain_ref, hshift_ref, rows_ref = refs[parts:]
    total = 0.0
    for d, ref in enumerate(part_refs):
        cut = ref.shape[0] - SMALL
        total = total + ref[cut:].astype(f32)
        at = 0 if parts == 1 else pl.multiple_of((lax.axis_index("seq") ^ d) * cut, cut)
        rows_ref[pl.ds(at, cut), :] = ref[0:cut].astype(f32)
    groups = up_ref.shape[2] // HALF
    base = groups * own + size
    late = late_ref[...].astype(f32)
    for g in range(groups):
        up_ref[0, :, g * HALF : (g + 1) * HALF] = rows_ref[g * own : (g + 1) * own]
        up_ref[1, :, g * HALF : (g + 1) * HALF] = late[g * own : (g + 1) * own]
    down_ref[0] = rows_ref[groups * own : base]
    down_ref[1] = late[groups * own : base]

    def joined(magnitude, phase, tail):
        return jnp.concatenate([magnitude, tail[:, 0:1], phase, tail[:, 1:2]], axis=1)

    tail = late[base + 2 * own :]
    head_ref[...] = joined(late[base : base + own], late[base + own : base + 2 * own], tail)
    bias = jnp.concatenate([tail[g : g + 1, EXTRA:] for g in range(3)], axis=1)
    hbias_ref[...] = joined(bias[:, :HALF], bias[:, HALF : 2 * HALF], bias[:, 2 * HALF :])

    width = total.shape[1]
    me = lax.axis_index("dp")

    def pick(values, count, base):
        at = lax.broadcasted_iota(jnp.int32, (width, count), 0)
        to = lax.broadcasted_iota(jnp.int32, (width, count), 1)
        place = jnp.where(at + base == to + me * count, 1.0, 0.0).astype(low)
        high = values.astype(low)
        rest = (values - high.astype(f32)).astype(low)
        return jnp.dot(high, place, preferred_element_type=f32) + jnp.dot(rest, place, preferred_element_type=f32)

    rows = pick(total[0:32], own, 0)
    for b in range(BLOCKS):
        dw_ref[:, b, :] = rows[KERNEL * b : KERNEL * (b + 1)]
        gains_ref[b] = rows[14 + 2 * b : 16 + 2 * b]
        biases_ref[:, b, :] = rows[18 + 3 * b : 21 + 3 * b]
    hgain_ref[...] = rows[24:25]
    hshift_ref[...] = rows[25:26]
    biases = jnp.zeros((2, size), f32)
    for g in range(groups):
        picked = [pick(total[26 + b * groups + g : 27 + b * groups + g], size, g * width) for b in range(BLOCKS)]
        biases = biases + jnp.concatenate(picked, axis=0)
    upb_ref[...] = biases


def pair_kernel(keep_ref, recv_ref, kept_ref, *sent_refs):
    kept_ref[...] = keep_ref[0].astype(f32) + recv_ref[0].astype(f32)
    for h, ref in enumerate(sent_refs):
        ref[...] = (keep_ref[h + 1].astype(f32) + recv_ref[h + 1].astype(f32)).astype(low)


def cross_kernel(count, kept_ref, *refs):
    recvs, outs, total_ref = refs[: len(refs) - count - 1], refs[len(refs) - count - 1 : -1], refs[-1]
    total = kept_ref[...]
    for ref in recvs:
        total = total + ref[...].astype(f32)
    total_ref[...] = total
    cut = kept_ref.shape[0] // count
    for d, ref in enumerate(outs):
        at = pl.multiple_of((lax.axis_index("seq") ^ d) * cut, cut)
        ref[...] = total_ref[pl.ds(at, cut), :].astype(ref.dtype)


def over_seq_kernel(*refs):
    small_ref, out_ref = refs[-2:]
    total = refs[0][...].astype(f32)
    for ref in refs[1:-2]:
        total = total + ref[...].astype(f32)
    cut = total.shape[0]
    out_ref[0:cut] = total.astype(low)
    small = small_ref[0].astype(f32)
    for i in range(1, small_ref.shape[0]):
        small = small + small_ref[i].astype(f32)
    out_ref[cut:] = small.astype(low)


def sum_kernel(*refs):
    total = refs[0][...].astype(f32)
    for ref in refs[1:-1]:
        total = total + ref[...].astype(f32)
    refs[-1][...] = total.astype(refs[-1].dtype)


def add_all(arrays, kind, name, after=(), us=0):
    return simple_call(sum_kernel, arrays, [(arrays[0].shape, kind)], name, after=after, us=us)[0]


def pair_stage(keep, recv, name, after=()):
    piece = keep.shape[1:]
    kept, *sent = simple_call(
        pair_kernel, [keep, recv], [(piece, f32)] + [(piece, low)] * (keep.shape[0] - 1), name, after=after
    )
    return kept, [swap(x, "dp", 2 * (h + 1)) for h, x in enumerate(sent)]


def summed_over(x, axis):
    bit = 1
    while bit < lax.axis_size(axis):
        x = x + swap(x, axis, bit)
        bit *= 2
    return x


def per_device(
    features,
    lengths,
    dw_weight,
    block_gains,
    block_biases,
    up_weight,
    up_bias,
    down_weight,
    head_gain,
    head_shift,
    head_weight,
    head_bias,
    audio_grad,
):
    count = lax.axis_size("dp")
    pairs = count // 2
    micro = features.shape[0]
    rows = features.shape[2]
    width = features.shape[3]
    units = up_weight.shape[2]
    ext = rows + 2 * HALO
    own = width // count
    size = units // count
    seq_count = lax.axis_size("seq")
    features = features[:, 0]
    audio_grad = audio_grad[:, 0]
    columns = 2 * HALF + EXTRA
    run = functools.partial(call, grid=micro, lengths=lengths)

    def edge(columns, at):
        return pl.BlockSpec((micro, HALO, columns), lambda i: (0, at, 0))

    last_at = rows // HALO - 1
    packed_ins = [
        dw_weight.swapaxes(0, 1),
        block_gains,
        block_biases.swapaxes(0, 1),
        up_bias,
        head_gain[None],
        head_shift[None],
        head_weight,
        up_weight,
        down_weight,
    ]
    packed_outs = [
        (micro, HALO, width + HOP),
        (micro, HALO, width + HOP),
        (own + 16, units),
        (units // HALF * own + size + 3 * own, HALF),
    ]

    def whole_block(dims):
        return pl.BlockSpec(tuple(dims), lambda i: (0,) * len(dims))

    first, last, up0_piece, rest_piece = pl.pallas_call(
        pack_kernel,
        grid=(1,),
        in_specs=[edge(width, 0), edge(width, last_at), edge(HOP, 0), edge(HOP, last_at)]
        + [whole_block(a.shape) for a in packed_ins],
        out_specs=[whole_block(dims) for dims in packed_outs],
        out_shape=[jax.ShapeDtypeStruct(dims, low) for dims in packed_outs],
        compiler_params=pltpu.CompilerParams(vmem_limit_bytes=60 * MiB),
        cost_estimate=cost(0),
        name="pack",
    )(features, features, audio_grad, audio_grad, *packed_ins)
    before = lax.ppermute(last, "seq", [(i, i + 1) for i in range(seq_count - 1)])
    after = lax.ppermute(first, "seq", [(i + 1, i) for i in range(seq_count - 1)])
    rest = lax.all_gather(rest_piece, "dp", axis=0)
    squared = jnp.asarray((window_values() ** 2).reshape(4, HOP), f32)
    tables = jnp.asarray(head_tables())

    def shape(columns):
        return (micro, ext, columns)

    def dma(*size):
        return pltpu.SemaphoreType.DMA(size or (count,))

    def across(x):
        return [x] + [swap(x, "dp", d) for d in range(2, count, 2)]

    def stacked(pieces, name, after, following=None):
        piece = pieces[0].shape
        ins = pieces + ([] if following is None else [following[0]])
        outs = [((pairs,) + piece, low)] + ([] if following is None else [(following[0].shape[1:], low)])
        if following is None:
            (even,) = simple_call(functools.partial(gather_kernel, pairs, 0), ins, outs, name, after=after)
            return (even, swap(even, "dp", 1)), None
        even, piece = simple_call(functools.partial(gather_kernel, pairs, following[1]), ins, outs, name, after=after)
        return (even, swap(even, "dp", 1)), piece

    up0_pieces = across(up0_piece)
    table_grad, recip = run(
        functools.partial(dft_kernel, rows),
        ins=[(before, "rows"), (audio_grad, "rows"), (after, "rows"), (squared, "all"), (tables, "all")],
        outs=[(shape(NFFT), low, "rows"), ((ext, HOP), f32, "all")],
        scratch=[],
        us=20,
        name="dft",
    )
    up0, down0_piece = stacked(up0_pieces, "stack_up0", [recip], (down_weight, 0))
    down0_pieces = across(down0_piece)
    normed, unit, inv_std, taps, vec, upb, bias_row_all = run(
        functools.partial(conv_kernel, rows, own, units),
        ins=[(before, "rows"), (features, "rows"), (after, "rows"), (head_bias[None], "all"), (up0[0], "any"), (up0[1], "any")],
        outs=[
            (shape(width), low, "rows"),
            (shape(width), low, "rows"),
            (shape(1), f32, "rows"),
            ((16, width), f32, "all"),
            ((16, width), f32, "all"),
            ((16, units), f32, "all"),
            ((1, columns), f32, "all"),
        ],
        scratch=[pltpu.VMEM((count, 16, 512), low), pltpu.VMEM((ext + 16, width), f32), dma()],
        name="conv",
    )
    down0, _ = stacked(down0_pieces, "stack_down0", [taps])
    hidden, act, slope, branch = run(
        functools.partial(forward_kernel, rows, own, size),
        ins=[
            (before, "rows"),
            (features, "rows"),
            (after, "rows"),
            (normed, "rows"),
            (vec, "all"),
            (upb, "all"),
            (up0[0], "any"),
            (up0[1], "any"),
            (down0[0], "any"),
            (down0[1], "any"),
        ],
        outs=[(shape(width), f32, "rows"), (shape(units), low, "rows"), (shape(units), low, "rows"), (shape(width), low, "rows")],
        scratch=[pltpu.VMEM((width, units), low), pltpu.VMEM((units, width), low), dma(), dma()],
        name="forward",
    )
    grouped = units // HALF * own
    packed = 3 * own + size + grouped
    audio, incoming, keep1, send1, small_mid, sbias1 = run(
        functools.partial(middle_kernel, rows, own, size),
        ins=[
            (hidden, "rows"),
            (table_grad, "rows"),
            (recip, "all"),
            (taps, "all"),
            (vec, "all"),
            (upb, "all"),
            (bias_row_all, "all"),
            (tables, "any"),
            (rest, "any"),
        ],
        outs=[
            ((micro, rows, HOP), f32, "rows"),
            (shape(width), f32, "rows"),
            ((pairs, packed, HALF), low, "all"),
            ((pairs, packed, HALF), low, "all"),
            ((16, width), f32, "all"),
            ((1, units), f32, "all"),
        ],
        scratch=[
            pltpu.VMEM((NFFT, NFFT), low),
            pltpu.VMEM((width, units), low),
            pltpu.VMEM((units, width), low),
            pltpu.VMEM((width, columns), low),
            pltpu.VMEM((width, columns), f32),
            pltpu.VMEM((width, units), f32),
            pltpu.VMEM((units, width), f32),
            pltpu.VMEM((ext, units), low),
            pltpu.VMEM((ext, units), low),
            pltpu.VMEM((ext + 16, width), f32),
            pltpu.VMEM((ext + 16, width), f32),
            pltpu.VMEM((ext + 16, NFFT), f32),
            pltpu.VMEM((ext, width), f32),
            pltpu.VMEM((ext, width), f32),
            pltpu.VMEM((ext, 1), f32),
            pltpu.VMEM((ext, 1), f32),
            pltpu.VMEM((ext, width), low),
            pltpu.VMEM((ext, width), low),
            pltpu.VMEM((width, rows), low),
            pltpu.VMEM((ext, width), low),
            pltpu.VMEM((ext, width), low),
            pltpu.VMEM((ext, NFFT), low),
            pltpu.VMEM((ext, columns), low),
            pltpu.VMEM((128, width), f32),
            pltpu.VMEM((8, units), f32),
            pltpu.VMEM((8, columns), f32),
            dma(count, 5 + units // HALF),
        ],
        name="middle",
        limit=56,
    )
    kept1, recvs1 = pair_stage(keep1, swap(send1, "dp", 1), "late_pair")
    pre_grad, keep, send, small_down, sbias0 = run(
        functools.partial(back_down_kernel, rows, own, size),
        ins=[
            (incoming, "rows"),
            (branch, "rows"),
            (act, "rows"),
            (slope, "rows"),
            (normed, "rows"),
            (vec, "all"),
            (down0[0], "any"),
            (down0[1], "any"),
        ],
        outs=[
            (shape(units), low, "rows"),
            ((pairs, grouped + size, width), low, "all"),
            ((pairs, grouped + size, width), low, "all"),
            ((8, width), f32, "all"),
            ((1, units), f32, "all"),
        ],
        scratch=[
            pltpu.VMEM((units, width), low),
            pltpu.VMEM((units, width), f32),
            pltpu.VMEM((width, units), f32),
            pltpu.VMEM((ext, width), low),
            pltpu.VMEM((64, width), f32),
            pltpu.VMEM((8, units), f32),
            dma(),
        ],
        after=[kept1],
        us=20,
        name="back_down",
    )
    shard1 = add_all([kept1] + recvs1, low, "late_cross", after=[sbias0], us=200)
    late = lax.psum(shard1, "seq")
    kept, recvs = pair_stage(keep, swap(send, "dp", 1), "pair", after=[shard1])
    feature_grad, small_conv = run(
        functools.partial(back_up_kernel, rows, own),
        ins=[
            (pre_grad, "rows"),
            (unit, "rows"),
            (inv_std, "rows"),
            (features, "rows"),
            (incoming, "rows"),
            (taps, "all"),
            (vec, "all"),
            (up0[0], "any"),
            (up0[1], "any"),
        ],
        outs=[((micro, rows, width), f32, "rows"), ((16, width), f32, "all")],
        scratch=[pltpu.VMEM((width, units), low), pltpu.VMEM((ext + 16, width), f32), pltpu.VMEM((128, width), f32), dma()],
        after=[kept],
        name="back_up",
    )
    (smalls,) = simple_call(
        small_kernel, [small_conv, small_down, sbias0, small_mid, sbias1], [((SMALL, width), low)], "small"
    )
    cut = kept.shape[0] // seq_count
    small_all = lax.all_gather(smalls, "dp", axis=0)
    if cut % 16:
        own_sum = add_all([kept] + recvs, f32, "cross", after=[smalls])
        sent = own_sum.astype(low)
        whole = add_all([own_sum] + [swap(sent, "seq", d) for d in range(1, seq_count)], low, "over_seq")
        small = jnp.sum(small_all.astype(f32), axis=0).astype(low)
        small = add_all([small] + [swap(small, "seq", d) for d in range(1, seq_count)], low, "small_seq")
        parts = [jnp.concatenate([whole, small], axis=0)]
    else:
        pieces = simple_call(
            functools.partial(cross_kernel, seq_count),
            [kept] + recvs,
            [((cut, width), f32)] + [((cut, width), low)] * (seq_count - 1),
            "cross",
            scratch=[pltpu.VMEM(kept.shape, f32)],
            after=[smalls],
        )
        part = simple_call(
            over_seq_kernel,
            [pieces[0]] + [swap(pieces[d], "seq", d) for d in range(1, seq_count)] + [small_all],
            [((cut + SMALL, width), low)],
            "over_seq",
        )[0]
        parts = [part] + [swap(part, "seq", d) for d in range(1, seq_count)]
    outs = simple_call(
        functools.partial(final_kernel, own, size, len(parts)),
        [late] + parts,
        [
            ((BLOCKS, own, units), f32),
            ((BLOCKS, size, width), f32),
            ((own, 2 * BINS), f32),
            ((1, 2 * BINS), f32),
            ((KERNEL, BLOCKS, own), f32),
            ((BLOCKS, 2, own), f32),
            ((3, BLOCKS, own), f32),
            ((BLOCKS, size), f32),
            ((1, own), f32),
            ((1, own), f32),
        ],
        "final",
        scratch=[pltpu.VMEM(kept.shape, f32)],
    )
    up_grad, down_grad, head_grad, bias_grad, dw_grad, gains_grad, biases_grad, up_bias_grad, hgain_grad, hshift_grad = outs
    return (
        audio[:, None],
        feature_grad[:, None],
        dw_grad.swapaxes(0, 1),
        gains_grad,
        biases_grad.swapaxes(0, 1),
        up_grad,
        up_bias_grad,
        down_grad,
        hgain_grad[0],
        hshift_grad[0],
        head_grad,
        bias_grad[0],
    )


def solution(mesh):
    return jax.shard_map(
        per_device,
        mesh=mesh,
        in_specs=(
            P(None, "dp", "seq", None),
            P(None, "dp"),
            P(None, None, "dp"),
            P(None, None, "dp"),
            P(None, None, "dp"),
            P(None, "dp", None),
            P(None, "dp"),
            P(None, "dp", None),
            P("dp"),
            P("dp"),
            P("dp", None),
            P(),
            P(None, "dp", "seq", None),
        ),
        out_specs=(
            P(None, "dp", "seq", None),
            P(None, "dp", "seq", None),
            P(None, None, "dp"),
            P(None, None, "dp"),
            P(None, None, "dp"),
            P(None, "dp", None),
            P(None, "dp"),
            P(None, "dp", None),
            P("dp"),
            P("dp"),
            P("dp", None),
            P(),
        ),
        check_vma=False,
    )
```

```python
import functools
import math

import jax
import jax.numpy as jnp
import numpy as np
from jax import lax
from jax.experimental import pallas as pl
from jax.experimental.pallas import tpu as pltpu
from jax.sharding import PartitionSpec as P

NFFT = 1024
HOP = 256
BINS = 513
HALF = 512
EXTRA = 128
KERNEL = 7
BLOCKS = 2
HALO = 16
SMALL = 32
norm_eps = 1e-06
f32 = jnp.float32
low = jnp.bfloat16
rows_dims = (((0,), (0,)), ((), ()))
cols_dims = (((1,), (1,)), ((), ()))
MiB = 2**20
GELU = (0.7978202661111929, 0.03654664812915587, -0.00019444764679970054, -1.3688682486738934e-05)
SIN = (6.283184921107194, -41.34159015596926, 81.59997289449204, -76.61480381354174, 41.34439732745281, -12.473668162531846)
COS = (0.9999992215705861, -19.738982516102407, 64.92872660899411, -85.27239689575316, 58.79403819232432, -21.076781286284348)


def window_values():
    return 0.5 - 0.5 * np.cos(np.arange(NFFT) * (2.0 * math.pi / NFFT))


def head_tables():
    row = np.arange(NFFT)
    frequency = np.where(row < HALF, row, np.where(row == HALF, HALF, row - HALF))
    angles = (frequency[:, None] * np.arange(NFFT)[None, :] % NFFT) * (2.0 * math.pi / NFFT)
    weight = np.where((row == 0) | (row == HALF), 1.0, 2.0)[:, None] / NFFT
    values = np.where((row <= HALF)[:, None], np.cos(angles), -np.sin(angles)) * weight
    return (values * window_values()[None, :]).astype(jnp.bfloat16)


def swap(x, axis, d):
    return lax.ppermute(x, axis, [(i, i ^ d) for i in range(lax.axis_size(axis))])


def poly(z, coefficients):
    p = coefficients[-1]
    for c in coefficients[-2::-1]:
        p = p * z + c
    return p


def gelu_parts(x):
    u = jnp.clip(x, -5.2, 5.2)
    z = u * u
    p = poly(z, [jnp.asarray(c, x.dtype) for c in GELU])
    half = jnp.asarray(0.5, x.dtype)
    cumulative = half * jnp.tanh(u * p) + half
    density = jnp.exp2(z * jnp.asarray(-0.5 * math.log2(math.e), x.dtype))
    return x * cumulative, cumulative + (x * jnp.asarray(1.0 / math.sqrt(2.0 * math.pi), x.dtype)) * density


def norm_parts(values):
    centred = values - jnp.mean(values, axis=1, keepdims=True)
    inv_std = lax.rsqrt(jnp.mean(centred * centred, axis=1, keepdims=True) + norm_eps)
    return centred * inv_std, inv_std


def norm_back(normed_grad, unit, inv_std, gain):
    unit_grad = normed_grad * gain
    inner = jnp.mean(unit_grad * unit, axis=1, keepdims=True)
    return inv_std * (unit_grad - jnp.mean(unit_grad, axis=1, keepdims=True) - unit * inner)


def total_rows(x):
    return jnp.sum(x, axis=0, keepdims=True)


def row(ref, i):
    return ref[i : i + 1]


def turns(x):
    r = x * (1.0 / (2.0 * math.pi))
    r = r - jnp.floor(r + 0.5)
    z = r * r
    return poly(z, COS), r * poly(z, SIN)


class Frames:
    def __init__(self, rows, lengths_ref):
        self.rows = rows
        self.ext = rows + 2 * HALO
        self.own = slice(HALO, HALO + rows)
        self.start = lax.axis_index("seq") * rows - HALO
        self.total = rows * lax.axis_size("seq")
        self.length = lengths_ref[pl.program_id(0), 0]
        self.tiles = [(0, HALO)] + [(r, 64) for r in range(HALO, HALO + rows, 64)] + [(HALO + rows, HALO)]
        self.half = self.ext // 2

    def at(self, r=0, n=None):
        return lax.broadcasted_iota(jnp.int32, (n or self.ext, 1), 0) + (self.start + r)

    def inside(self, r=0, n=None):
        t = self.at(r, n)
        return (t >= 0) & (t < self.total)

    def mask(self, r=0, n=None):
        t = self.at(r, n)
        return (t >= 0) & (t < self.total) & (t < self.length)

    def owns(self, r):
        return HALO <= r < HALO + self.rows

    def parts(self):
        return [(r0, range(r0, r0 + self.half, 16)) for r0 in (0, self.half)]


def feature_tile(frames, before_ref, features_ref, after_ref, r, n):
    width = features_ref.shape[2]
    if r < HALO:
        tile = before_ref[0, r : r + n, :width]
    elif r < HALO + frames.rows:
        tile = features_ref[0, r - HALO : r - HALO + n]
    else:
        tile = after_ref[0, r - HALO - frames.rows : r - HALO - frames.rows + n, :width]
    return jnp.where(frames.mask(r, n), tile.astype(f32), 0.0)


def fold(x):
    total = x[0:8]
    for r in range(8, x.shape[0], 8):
        total = total + x[r : r + 8]
    return total


def add_to(ref, i, x):
    ref[8 * i : 8 * i + 8] += fold(x)


def assemble(even_ref, odd_ref, base, size, whole_ref, sems):
    me = lax.axis_index("dp")
    copies = []
    for h in range(even_ref.shape[0]):
        for c, ref in enumerate((even_ref, odd_ref)):
            at = pl.multiple_of((me ^ (2 * h + c)) * size, size)
            for g in range(whole_ref.shape[1] // HALF):
                copies.append(
                    pltpu.make_async_copy(
                        ref.at[h, pl.ds(base + g * size, size)],
                        whole_ref.at[pl.ds(at, size), pl.ds(g * HALF, HALF)],
                        sems.at[2 * h + c, g],
                    )
                )
    return copies


def run_copies(copies):
    for copy in copies:
        copy.start()
    for copy in copies:
        copy.wait()


def skipping(kernel, start, count):
    def inner(*refs):
        return kernel(*refs[:start], *refs[start + count :])

    return inner if count else kernel


def in_hbm(x):
    return pltpu.with_memory_space_constraint(x, pltpu.HBM)


def cost(us):
    return pl.CostEstimate(flops=1000 + int(us * 1e9), bytes_accessed=1000, transcendentals=0)


def call(kernel, grid, lengths, ins, outs, scratch, name, after=(), limit=48, us=0):
    def spec(shape, kind):
        if isinstance(kind, pl.BlockSpec):
            return kind
        if kind == "any":
            return pl.BlockSpec(memory_space=pl.ANY)
        if kind == "rows":
            return pl.BlockSpec((1,) + tuple(shape[1:]), lambda i, s: (i,) + (0,) * (len(shape) - 1))
        return pl.BlockSpec(tuple(shape), lambda i, s: (0,) * len(shape))

    kernel = skipping(kernel, 1 + len(ins), len(after))
    ins = ins + [(a, "any") for a in after]
    return pl.pallas_call(
        kernel,
        out_shape=[(pltpu.HBM if kind == "rows" or len(s) == 3 else jax.ShapeDtypeStruct)(tuple(s), d) for s, d, kind in outs],
        grid_spec=pltpu.PrefetchScalarGridSpec(
            num_scalar_prefetch=1,
            grid=(grid,),
            in_specs=[spec(a.shape, kind) for a, kind in ins],
            out_specs=[spec(s, kind) for s, _, kind in outs],
            scratch_shapes=scratch,
        ),
        compiler_params=pltpu.CompilerParams(vmem_limit_bytes=limit * MiB, dimension_semantics=("arbitrary",)),
        cost_estimate=cost(us),
        name=name,
    )(lengths, *[in_hbm(a) if kind == "rows" and a.shape[1] != HALO else a for a, kind in ins])


def simple_call(kernel, ins, outs, name, scratch=(), after=(), limit=16, us=0, hbm=(), out_hbm=False):
    whole = pl.BlockSpec(memory_space=pltpu.VMEM)
    return pl.pallas_call(
        skipping(kernel, len(ins), len(after)),
        out_shape=[(pltpu.HBM if out_hbm else jax.ShapeDtypeStruct)(tuple(s), d) for s, d in outs],
        in_specs=[whole] * len(ins) + [pl.BlockSpec(memory_space=pl.ANY)] * len(after),
        out_specs=[whole] * len(outs),
        scratch_shapes=list(scratch),
        compiler_params=pltpu.CompilerParams(vmem_limit_bytes=limit * MiB),
        cost_estimate=cost(us),
        name=name,
    )(*[in_hbm(a) if i in hbm else a for i, a in enumerate(ins)], *after)


def head_columns(x):
    lane = lax.broadcasted_iota(jnp.int32, (x.shape[0], EXTRA), 1)
    tail = jnp.where(lane == 0, x[:, BINS - 1 : BINS], jnp.where(lane == 1, x[:, 2 * BINS - 1 :], 0.0))
    return x[:, : BINS - 1], x[:, BINS : 2 * BINS - 1], tail


def pack_kernel(
    first_ref, last_ref, gfirst_ref, glast_ref, dw_ref, gains_ref, biases_ref, upb_ref, hgain_ref, hshift_ref,
    head_ref, up_ref, down_ref, first_out, last_out, small_out, rest_out,
):
    width = first_ref.shape[2]
    first_out[:, :, :width] = first_ref[...]
    first_out[:, :, width:] = gfirst_ref[...].astype(low)
    last_out[:, :, :width] = last_ref[...]
    last_out[:, :, width:] = glast_ref[...].astype(low)
    own = up_ref.shape[1]
    small_out[...] = jnp.zeros(small_out.shape, low)

    def stack(parts):
        parts = [p.astype(f32) for p in parts]
        filled = sum(p.shape[0] for p in parts)
        return jnp.concatenate(parts + [jnp.zeros((16 - filled, parts[0].shape[1]), f32)], axis=0).astype(low)

    def halves(x):
        high = x.astype(low).astype(f32)
        return [high, x - high]

    small_out[:, 0:own] = stack([dw_ref[:, 0, :], dw_ref[:, 1, :]])
    small_out[:, 128 : 128 + own] = stack(
        [gains_ref[0], gains_ref[1], biases_ref[:, 0, :], biases_ref[:, 1, :]] + halves(hgain_ref[...]) + halves(hshift_ref[...])
    )
    small_out[:, 256 : 256 + upb_ref.shape[1]] = stack([upb_ref[...]])
    size = down_ref.shape[1]
    base = up_ref.shape[2] // HALF * own
    for g in range(0, up_ref.shape[2], HALF):
        rest_out[g // HALF * own : (g // HALF + 1) * own] = up_ref[1, :, g : g + HALF]
    rest_out[base : base + size] = down_ref[1]
    size = base + size

    magnitude, phase, tail = head_columns(head_ref[...])
    rest_out[size : size + own] = magnitude.astype(low)
    rest_out[size + own : size + 2 * own] = phase.astype(low)
    rest_out[size + 2 * own :] = jnp.zeros((own, HALF), low)
    rest_out[size + 2 * own :, :EXTRA] = tail.astype(low)


def dft_kernel(rows, lengths, before_ref, grad_ref, after_ref, squared_ref, table_ref, out_ref, recip_ref):
    frames = Frames(rows, lengths)
    width = before_ref.shape[2] - HOP

    @pl.when(pl.program_id(0) == 0)
    def _():
        envelope = jnp.zeros((frames.ext, HOP), f32)
        for q in range(4):
            source = frames.at() + (2 - q)
            valid = (source >= 0) & (source < frames.total)
            envelope = envelope + jnp.where(valid, row(squared_ref, q), 0.0)
        recip_ref[...] = jnp.where(frames.inside(), 1.0 / envelope, 0.0)

    whole = jnp.concatenate(
        [before_ref[0, :, width:].astype(f32), grad_ref[0], after_ref[0, :, width:].astype(f32)], axis=0
    )
    own = jnp.where(frames.mask(), whole * recip_ref[...], 0.0)
    parts = [own if q == 2 else pltpu.roll(own, (2 - q) % frames.ext, 0) for q in range(4)]
    framed = jnp.where(frames.inside(), jnp.concatenate(parts, axis=1), 0.0).astype(low)
    out_ref[0] = lax.dot_general(framed, table_ref[...], cols_dims, preferred_element_type=f32).astype(low)


def put_padded(pad_ref, frames, tile_of):
    zeros = jnp.zeros((8, pad_ref.shape[1]), f32)
    pad_ref[0:8] = zeros
    pad_ref[frames.ext + 8 :] = zeros
    for r, n in frames.tiles:
        pad_ref[8 + r : 8 + r + n] = tile_of(r, n)


def conv_tile(pad_ref, r, n, taps_ref, base, bias):
    window = pad_ref[r : r + n + 16]
    conv = bias + row(taps_ref, base + 3) * window[8 : 8 + n]
    for k in range(KERNEL):
        if k != 3:
            conv = conv + row(taps_ref, base + k) * pltpu.roll(window, (3 - k) % (n + 16), 0)[8 : 8 + n]
    return conv


def conv_norm(frames, pad_ref, taps_ref, base, vec_ref, b, unit_at, inv_at, normed_at):
    for r, n in frames.tiles:
        unit, inv_std = norm_parts(conv_tile(pad_ref, r, n, taps_ref, base, bias_row(vec_ref, b, 0)))
        unit_at[r : r + n] = unit.astype(unit_at.dtype)
        inv_at[r : r + n] = inv_std
        normed_at[r : r + n] = (unit * gain_row(vec_ref, b, 0) + bias_row(vec_ref, b, 1)).astype(low)


def gain_row(ref, b, i):
    return row(ref, 2 * b + i)


def bias_row(ref, b, i):
    return row(ref, 4 + 3 * b + i)


def conv_kernel(
    rows, own, units, lengths, before_ref, features_ref, after_ref, hbias_ref, even_ref, odd_ref,
    normed_ref, unit_ref, inv_ref, masked_ref, taps_ref, vec_ref, upb_ref, bias_ref, small_ref, pad_ref, sems,
):
    @pl.when(pl.program_id(0) == 0)
    def _():
        me = lax.axis_index("dp")
        count = 2 * even_ref.shape[0]
        copies = []
        for d in range(count):
            ref = odd_ref if d % 2 else even_ref
            copies.append(
                pltpu.make_async_copy(ref.at[d // 2], small_ref.at[d], sems.at[d])
            )
        run_copies(copies)

        def spread(lanes, size, out_ref):
            total = jnp.zeros(out_ref.shape, f32)
            at = lax.broadcasted_iota(jnp.int32, (size, out_ref.shape[1]), 0)
            to = lax.broadcasted_iota(jnp.int32, (size, out_ref.shape[1]), 1)
            for d in range(count):
                place = jnp.where(to == at + (me ^ d) * size, 1.0, 0.0).astype(low)
                total = total + jnp.dot(small_ref[d, :, lanes : lanes + size], place, preferred_element_type=f32)
            out_ref[...] = total

        spread(0, own, taps_ref)
        spread(128, own, vec_ref)
        spread(256, units // count, upb_ref)
        magnitude, phase, tail = head_columns(hbias_ref[...])
        bias_ref[:, :HALF] = magnitude
        bias_ref[:, HALF : 2 * HALF] = phase
        bias_ref[:, 2 * HALF :] = tail

    frames = Frames(rows, lengths)
    put_padded(pad_ref, frames, functools.partial(feature_tile, frames, before_ref, features_ref, after_ref))
    masked_ref[0] = pad_ref[8 : 8 + frames.ext].astype(low)
    conv_norm(frames, pad_ref, taps_ref, 0, vec_ref, 0, unit_ref.at[0], inv_ref.at[0], normed_ref.at[0])


def gelu_rows(normed, weight_ref, bias, act_at, slope_at, rows, chunk=256):
    for c in range(0, weight_ref.shape[1], chunk):
        pre = jnp.dot(normed, weight_ref[:, c : c + chunk], preferred_element_type=f32) + bias[:, c : c + chunk]
        act, slope = gelu_parts(pre.astype(low))
        act_at[rows, c : c + chunk] = act
        slope_at[rows, c : c + chunk] = slope


def up_gelu(frames, normed_at, weight_ref, bias, act_at, slope_at):
    for r0, _ in frames.parts():
        part = slice(r0, r0 + frames.half)
        gelu_rows(normed_at[part], weight_ref, bias, act_at, slope_at, part)


def forward_kernel(
    own, size, lengths, masked_ref, normed_ref, vec_ref, upb_ref, even_ref, odd_ref,
    hidden_ref, act_ref, slope_ref, branch_ref, up_ref, down_ref, sems, sems2,
):
    first = pl.program_id(0) == 0
    ups = assemble(even_ref, odd_ref, 0, own, up_ref, sems)
    downs = assemble(even_ref, odd_ref, up_ref.shape[1] // HALF * own, size, down_ref, sems2)

    @pl.when(first)
    def _():
        for copy in ups + downs:
            copy.start()
        for copy in ups:
            copy.wait()

    act_at = act_ref.at[0]
    gelu_rows(normed_ref[0], up_ref, row(upb_ref, 0), act_at, slope_ref.at[0], slice(0, act_at.shape[0]))

    @pl.when(first)
    def _():
        for copy in downs:
            copy.wait()

    product = jnp.dot(act_at[...], down_ref[...], preferred_element_type=f32)
    for r in range(0, product.shape[0], 16):
        branch = product[r : r + 16] + bias_row(vec_ref, 0, 2)
        branch_ref[0, r : r + 16] = branch.astype(low)
        hidden_ref[0, r : r + 16] = masked_ref[0, r : r + 16].astype(f32) + gain_row(vec_ref, 0, 1) * branch


def split_rows(total_at, size, keep_at, send_at, pieces):
    me = lax.axis_index("dp")
    for h in range(pieces):
        at = pl.multiple_of((me ^ (2 * h)) * size, size)
        keep_at(h, total_at(pl.ds(at, size)).astype(low))
        at = pl.multiple_of((me ^ (2 * h + 1)) * size, size)
        send_at(h, total_at(pl.ds(at, size)).astype(low))


def give(ref, base):
    def put(h, value):
        ref[h, base : base + value.shape[0], : value.shape[1]] = value

    return put


def split_columns(total_ref, base, size, keep_ref, send_ref):
    for g in range(0, total_ref.shape[1], HALF):
        stop = min(g + HALF, total_ref.shape[1])
        at = base + g // HALF * size
        split_rows(lambda r: total_ref[r, g:stop], size, give(keep_ref, at), give(send_ref, at), keep_ref.shape[0])


def branch_tile(frames, r, hgrad, branch, gain, bgrad_at, sums_ref, at):
    bgrad = (gain * hgrad).astype(low)
    bgrad_at[r : r + 16] = bgrad
    if frames.owns(r):
        add_to(sums_ref, at, hgrad * branch.astype(f32))
        add_to(sums_ref, at + 1, bgrad.astype(f32))


def back_down(frames, bgrad_at, act_at, slope_at, weight_ref, total_ref, pgrad_at, chunk=512):
    own = frames.own
    for c in range(0, weight_ref.shape[0], chunk):
        part = slice(c, c + chunk)
        for r0, tiles in frames.parts():
            act_grad = lax.dot_general(bgrad_at[r0 : r0 + frames.half], weight_ref[part], cols_dims, preferred_element_type=f32)
            for r in tiles:
                grad = (act_grad[r - r0 : r - r0 + 16] * slope_at[r : r + 16, part].astype(f32)).astype(low)
                pgrad_at[r : r + 16, part] = grad
        total_ref[part] += lax.dot_general(act_at[own, part], bgrad_at[own], rows_dims, preferred_element_type=f32)


def back_up_norm(frames, pgrad_at, unit_at, inv_at, gain, weight_ref, put, sums_ref):
    for r0, tiles in frames.parts():
        product = lax.dot_general(pgrad_at[r0 : r0 + frames.half], weight_ref[...], cols_dims, preferred_element_type=f32)
        for r in tiles:
            normed_grad = product[r - r0 : r - r0 + 16]
            unit = unit_at[r : r + 16].astype(f32)
            conv_grad = norm_back(normed_grad, unit, inv_at[r : r + 16], gain)
            if frames.owns(r):
                conv_grad = conv_grad.astype(low).astype(f32)
                add_to(sums_ref, 7, conv_grad)
                add_to(sums_ref, 8, normed_grad * unit)
                add_to(sums_ref, 9, normed_grad)
            else:
                conv_grad = jnp.where(frames.inside(r, 16), conv_grad, 0.0).astype(low).astype(f32)
            put(r, conv_grad)


def conv_back_tile(frames, r, n, pad_ref, block_in_of, hgrad, taps_ref, base, sums_ref):
    window = pad_ref[r : r + n + 16]
    owns = frames.owns(r)
    block_in = block_in_of(r, n) if owns else None
    for k in range(KERNEL):
        moved = (window if k == 3 else pltpu.roll(window, (k - 3) % (n + 16), 0))[8 : 8 + n]
        hgrad = hgrad + row(taps_ref, base + k) * moved
        if owns:
            add_to(sums_ref, k, block_in * moved)
    return hgrad


def close_sums(sums_ref, small_ref):
    for i in range(sums_ref.shape[0] // 8):
        small_ref[i : i + 1] = total_rows(sums_ref[8 * i : 8 * i + 8])


def middle_kernel(
    rows, own, size, lengths, h_ref, tgrad_ref, recip_ref, taps_ref, vec_ref, upb_ref, bias_ref,
    table_hbm, rest_ref,
    audio_ref, hgrad_ref, cgrad_ref, keep_ref, send_ref, small_ref, sbias_ref,
    table_ref, up_ref, down_ref, head_ref, head_total, up_total, down_total, act_ref, slope_ref,
    pad_ref, frame_ref, unit1_ref, unit2_ref, inv1_ref, inv2_ref, normed1_ref, normed2_ref, turned_ref,
    branch_ref, bgrad_ref, spectrum_ref, lgrad_ref, sums_ref, sems,
):
    step = pl.program_id(0)

    copies = []
    groups = up_ref.shape[1] // HALF
    width = up_ref.shape[0]
    places = [(g * own, own, up_ref, g * HALF, HALF) for g in range(groups)]
    places.append((groups * own, size, down_ref, 0, HALF))
    base = groups * own + size
    places += [(base + g * own, own, head_ref, g * HALF, lanes) for g, lanes in enumerate((HALF, HALF, EXTRA))]
    for j in range(rest_ref.shape[0]):
        for i, (at, many, ref, lane, lanes) in enumerate(places):
            copy = pltpu.make_async_copy(
                rest_ref.at[j, pl.ds(at, many), pl.ds(0, lanes)],
                ref.at[pl.ds(j * many, many), pl.ds(lane, lanes)],
                sems.at[j, i],
            )
            copies.append((copy, i))
    copies.append((pltpu.make_async_copy(table_hbm, table_ref, sems.at[0, len(places)]), len(places)))
    copies.sort(key=lambda pair: pair[1])

    @pl.when(step == 0)
    def _():
        for copy, _ in copies:
            copy.start()
        for ref in (head_total, up_total, down_total, sums_ref):
            ref[...] = jnp.zeros_like(ref)
        turned_ref[width:] = jnp.ones((16, rows), low)
        for copy, _ in copies:
            copy.wait()

    frames = Frames(rows, lengths)
    mine, half, ext = frames.own, frames.half, frames.ext

    def block_in_tile(r, n):
        return jnp.where(frames.inside(r, n), h_ref[0, r : r + n], 0.0).astype(low).astype(f32)

    put_padded(pad_ref, frames, block_in_tile)
    conv_norm(frames, pad_ref, taps_ref, KERNEL, vec_ref, 1, unit1_ref, inv1_ref, normed1_ref)
    up_gelu(frames, normed1_ref, up_ref, row(upb_ref, 1), act_ref, slope_ref)

    head_gain = row(vec_ref, 10) + row(vec_ref, 11)
    head_shift = row(vec_ref, 12) + row(vec_ref, 13)
    for r0, tiles in frames.parts():
        product = jnp.dot(act_ref[r0 : r0 + half], down_ref[...], preferred_element_type=f32)
        for r in tiles:
            branch = product[r - r0 : r - r0 + 16] + bias_row(vec_ref, 1, 2)
            branch_ref[r : r + 16] = branch.astype(low)
            unit, inv_std = norm_parts(h_ref[0, r : r + 16] + gain_row(vec_ref, 1, 1) * branch)
            unit2_ref[r : r + 16] = unit
            inv2_ref[r : r + 16] = inv_std
            normed2_ref[r : r + 16] = (unit * head_gain + head_shift).astype(low)

    lane = lax.broadcasted_iota(jnp.int32, (16, EXTRA), 1)
    for r0, tiles in frames.parts():
        product = jnp.dot(normed2_ref[r0 : r0 + half], head_ref[...], preferred_element_type=f32)
        for r in tiles:
            logits = product[r - r0 : r - r0 + 16] + bias_ref[...]
            magnitude = jnp.exp(logits[:, :HALF])
            cos, sin = turns(logits[:, HALF : 2 * HALF])
            re = magnitude * cos
            im = magnitude * sin
            last = logits[:, 2 * HALF :]
            cos, sin = turns(pltpu.roll(last, EXTRA - 1, 1))
            top = jnp.exp(jnp.where(lane == 0, last, 0.0))
            top_re = top * cos
            top_im = top * sin
            spectrum_ref[r : r + 16, :HALF] = re.astype(low)
            spectrum_ref[r : r + 16, HALF : HALF + EXTRA] = jnp.where(lane == 0, top_re, im[:, :EXTRA]).astype(low)
            spectrum_ref[r : r + 16, HALF + EXTRA :] = im[:, EXTRA:].astype(low)
            tgrad = tgrad_ref[0, r : r + 16].astype(f32)
            re_grad = tgrad[:, :HALF]
            top_grad = tgrad[:, HALF : HALF + EXTRA]
            im_grad = jnp.concatenate([jnp.where(lane == 0, 0.0, top_grad), tgrad[:, HALF + EXTRA :]], axis=1)
            log_last = jnp.where(lane == 0, top_grad * top_re, 0.0)
            phase_last = jnp.where(lane == 1, pltpu.roll(top_grad * top_im, 1, 1), 0.0)
            grads = (re_grad * re + im_grad * im, im_grad * re - re_grad * im, log_last - phase_last)
            for g, grad in enumerate(grads):
                part = slice(g * HALF, g * HALF + grad.shape[1])
                lgrad_ref[r : r + 16, part] = grad.astype(low)

    for r0, tiles in frames.parts():
        product = jnp.dot(spectrum_ref[r0 : r0 + half], table_ref[...], preferred_element_type=f32)
        for r in tiles:
            framed = product[r - r0 : r - r0 + 16]
            if not frames.owns(r):
                framed = jnp.where(frames.inside(r, 16), framed, 0.0)
            frame_ref[8 + r : 8 + r + 16] = framed

    hgrad_at = hgrad_ref.at[0]
    for r0, tiles in frames.parts():
        product = lax.dot_general(lgrad_ref[r0 : r0 + half], head_ref[...], cols_dims, preferred_element_type=f32)
        for r in tiles:
            normed_grad = product[r - r0 : r - r0 + 16]
            unit = unit2_ref[r : r + 16]
            hgrad = norm_back(normed_grad, unit, inv2_ref[r : r + 16], head_gain)
            hgrad_at[r : r + 16] = hgrad
            if frames.owns(r):
                add_to(sums_ref, 12, normed_grad * unit)
                add_to(sums_ref, 13, normed_grad)
            branch_tile(frames, r, hgrad, branch_ref[r : r + 16], gain_row(vec_ref, 1, 1), bgrad_ref, sums_ref, 10)

    def audio_tile(r, n):
        audio = frame_ref[8 + r : 8 + r + n, 2 * HOP : 3 * HOP]
        for q in (0, 1, 3):
            window = frame_ref[r : r + n + 16, q * HOP : (q + 1) * HOP]
            audio = audio + pltpu.roll(window, (q - 2) % (n + 16), 0)[8 : 8 + n]
        audio_ref[0, r - HALO : r - HALO + n] = jnp.where(frames.mask(r, n), audio * recip_ref[r : r + n], 0.0)

    def beside(chunks, tiles, dot_of, put, work):
        each = -(-len(tiles) // len(chunks))
        for i, part in enumerate(chunks):
            product = dot_of(part)
            for r, n in tiles[i * each : (i + 1) * each]:
                work(r, n)
            put(part, product)

    own_tiles = [tile for tile in frames.tiles if frames.owns(tile[0])]
    turned_ref[:width] = normed2_ref[mine].T

    def put_head(part, product):
        head_total[:, part] += product

    beside(
        [slice(c, c + 384) for c in range(0, head_total.shape[1], 384)],
        own_tiles,
        lambda part: jnp.dot(turned_ref[...], lgrad_ref[mine, part], preferred_element_type=f32),
        put_head,
        audio_tile,
    )

    back_down(frames, bgrad_ref, act_ref, slope_ref, down_ref, down_total, slope_ref)
    def put_conv(r, grad):
        cgrad_ref[0, r : r + 16] = grad.astype(low)

    back_up_norm(frames, slope_ref, unit1_ref, inv1_ref, gain_row(vec_ref, 1, 0), up_ref, put_conv, sums_ref)
    turned_ref[:width] = normed1_ref[mine].T

    for c in range(0, up_total.shape[1], 256):
        up_total[:, c : c + 256] += jnp.dot(turned_ref[...], slope_ref[mine, c : c + 256], preferred_element_type=f32)

    @pl.when(step == pl.num_programs(0) - 1)
    def _():
        close_sums(sums_ref, small_ref)
        sbias_ref[...] = up_total[width : width + 1]
        groups = up_ref.shape[1] // HALF * own
        split_columns(up_total, 0, own, keep_ref, send_ref)
        split_columns(down_total, groups, size, keep_ref, send_ref)
        base = groups + size
        bias = head_total[width : width + 1]
        block = jnp.concatenate([bias[:, g : g + 384] for g in (0, 384, 768)] + [jnp.zeros((13, 384), f32)], axis=0)
        for h in range(keep_ref.shape[0]):
            for ref in (keep_ref, send_ref):
                ref[h, base + 2 * own :] = jnp.zeros((own, HALF), low)
                ref[h, base + 2 * own : base + 2 * own + 16, EXTRA:] = block.astype(low)
        split_columns(head_total, base, own, keep_ref, send_ref)


def back_down_kernel(
    rows, own, size, lengths, head_ref, cgrad_ref, h_ref, taps_ref, branch_ref, act_ref, slope_ref, normed_ref, vec_ref,
    even_ref, odd_ref, pgrad_ref, hgrad_ref, keep_ref, send_ref, small_ref, sbias_ref, weight_ref, down_total, up_total, bgrad_ref, turned_ref, pad_ref, sums_ref, sems,
):
    step = pl.program_id(0)

    @pl.when(step == 0)
    def _():
        copies = assemble(even_ref, odd_ref, up_total.shape[1] // HALF * own, size, weight_ref, sems)
        for copy in copies:
            copy.start()
        for ref in (down_total, up_total, sums_ref):
            ref[...] = jnp.zeros_like(ref)
        turned_ref[normed_ref.shape[2] :] = jnp.ones((16, rows), low)
        for copy in copies:
            copy.wait()

    frames = Frames(rows, lengths)
    mine = frames.own
    put_padded(pad_ref, frames, lambda r, n: cgrad_ref[0, r : r + n].astype(f32))

    def block_in_tile(r, n):
        return jnp.where(frames.inside(r, n), h_ref[0, r : r + n], 0.0).astype(low).astype(f32)

    for r, n in frames.tiles:
        hgrad_ref[0, r : r + n] = conv_back_tile(
            frames, r, n, pad_ref, block_in_tile, head_ref[0, r : r + n], taps_ref, KERNEL, sums_ref
        )
    for r in range(0, frames.ext, 16):
        branch_tile(frames, r, hgrad_ref[0, r : r + 16], branch_ref[0, r : r + 16], gain_row(vec_ref, 0, 1), bgrad_ref, sums_ref, 8)
    back_down(frames, bgrad_ref, act_ref.at[0], slope_ref.at[0], weight_ref, down_total, pgrad_ref.at[0])
    width = normed_ref.shape[2]
    turned_ref[:width] = normed_ref[0, mine].T
    up_total[...] += jnp.dot(turned_ref[...], pgrad_ref[0, mine], preferred_element_type=f32)

    @pl.when(step == pl.num_programs(0) - 1)
    def _():
        close_sums(sums_ref, small_ref)
        sbias_ref[...] = up_total[width : width + 1]
        split_columns(up_total, 0, own, keep_ref, send_ref)
        split_columns(down_total, up_total.shape[1] // HALF * own, size, keep_ref, send_ref)


def back_up_kernel(
    rows, own, lengths, pgrad_ref, unit_ref, inv_ref, features_ref, hgrad_ref, taps_ref, vec_ref, even_ref, odd_ref,
    out_ref, small_ref, weight_ref, pad_ref, sums_ref, sems,
):
    step = pl.program_id(0)

    @pl.when(step == 0)
    def _():
        sums_ref[...] = jnp.zeros_like(sums_ref)
        run_copies(assemble(even_ref, odd_ref, 0, own, weight_ref, sems))

    frames = Frames(rows, lengths)
    zeros = jnp.zeros((8, pad_ref.shape[1]), f32)
    pad_ref[0:8] = zeros
    pad_ref[frames.ext + 8 :] = zeros

    def put_conv(r, grad):
        pad_ref[8 + r : 8 + r + 16] = grad

    back_up_norm(
        frames, pgrad_ref.at[0], unit_ref.at[0], inv_ref.at[0], gain_row(vec_ref, 0, 0), weight_ref, put_conv, sums_ref
    )

    def block_in_tile(r, n):
        return jnp.where(frames.mask(r, n), features_ref[0, r - HALO : r - HALO + n].astype(f32), 0.0)

    for r, n in frames.tiles:
        if frames.owns(r):
            hgrad = conv_back_tile(frames, r, n, pad_ref, block_in_tile, hgrad_ref[0, r : r + n], taps_ref, 0, sums_ref)
            out_ref[0, r - HALO : r - HALO + n] = jnp.where(frames.mask(r, n), hgrad, 0.0)

    @pl.when(step == pl.num_programs(0) - 1)
    def _():
        close_sums(sums_ref, small_ref)


def small_kernel(conv0_ref, down0_ref, bias0_ref, mid_ref, bias1_ref, out_ref):
    width = out_ref.shape[1]
    groups = [r[:, g : g + width] for r in (bias0_ref, bias1_ref) for g in range(0, r.shape[1], width)]
    rows = [
        conv0_ref[0:7], down0_ref[0:7],
        conv0_ref[8:9], down0_ref[8:9], mid_ref[8:9], mid_ref[10:11],
        conv0_ref[7:8], conv0_ref[9:10], down0_ref[9:10], mid_ref[7:8], mid_ref[9:10], mid_ref[11:12],
        mid_ref[12:14],
    ] + groups
    filled = 26 + len(groups)
    rows = rows + [jnp.zeros((out_ref.shape[0] - filled, width), f32)] * (filled < out_ref.shape[0])
    out_ref[...] = jnp.concatenate(rows, axis=0).astype(low)


def gather_kernel(*refs):
    for h, ref in enumerate(refs[:-1]):
        refs[-1][h] = ref[...]


def gather_first_kernel(*refs):
    up_ref, down_ref, stack_ref, piece_ref = refs[-4:]
    for h, ref in enumerate(refs[:-4]):
        stack_ref[h] = ref[...]
    own = up_ref.shape[1]
    for g in range(0, up_ref.shape[2], HALF):
        piece_ref[g // HALF * own : (g // HALF + 1) * own] = up_ref[0, :, g : g + HALF]
    piece_ref[up_ref.shape[2] // HALF * own :] = down_ref[0]


def final_kernel(
    own, size, parts, late_ref, *refs,
):
    part_refs = refs[:parts]
    up_ref, down_ref, head_ref, hbias_ref, dw_ref, gains_ref, biases_ref, upb_ref, hgain_ref, hshift_ref, rows_ref = refs[parts:]
    total = 0.0
    for d, ref in enumerate(part_refs):
        cut = ref.shape[0] - SMALL
        total = total + ref[cut:].astype(f32)
        at = 0 if parts == 1 else pl.multiple_of((lax.axis_index("seq") ^ d) * cut, cut)
        rows_ref[pl.ds(at, cut), :] = ref[0:cut].astype(f32)
    groups = up_ref.shape[2] // HALF
    base = groups * own + size
    late = late_ref[...].astype(f32)
    for g in range(groups):
        up_ref[0, :, g * HALF : (g + 1) * HALF] = rows_ref[g * own : (g + 1) * own]
        up_ref[1, :, g * HALF : (g + 1) * HALF] = late[g * own : (g + 1) * own]
    down_ref[0] = rows_ref[groups * own : base]
    down_ref[1] = late[groups * own : base]

    def joined(magnitude, phase, tail):
        return jnp.concatenate([magnitude, tail[:, 0:1], phase, tail[:, 1:2]], axis=1)

    tail = late[base + 2 * own :]
    head_ref[...] = joined(late[base : base + own], late[base + own : base + 2 * own], tail)
    bias = jnp.concatenate([tail[g : g + 1, EXTRA:] for g in range(3)], axis=1)
    hbias_ref[...] = joined(bias[:, :HALF], bias[:, HALF : 2 * HALF], bias[:, 2 * HALF :])

    width = total.shape[1]
    me = lax.axis_index("dp")

    def pick(values, count, base):
        at = lax.broadcasted_iota(jnp.int32, (width, count), 0)
        to = lax.broadcasted_iota(jnp.int32, (width, count), 1)
        place = jnp.where(at + base == to + me * count, 1.0, 0.0).astype(low)
        high = values.astype(low)
        rest = (values - high.astype(f32)).astype(low)
        return jnp.dot(high, place, preferred_element_type=f32) + jnp.dot(rest, place, preferred_element_type=f32)

    rows = pick(total[0:32], own, 0)
    for b in range(BLOCKS):
        dw_ref[:, b, :] = rows[KERNEL * b : KERNEL * (b + 1)]
        gains_ref[b] = rows[14 + 2 * b : 16 + 2 * b]
        biases_ref[:, b, :] = rows[18 + 3 * b : 21 + 3 * b]
    hgain_ref[...] = rows[24:25]
    hshift_ref[...] = rows[25:26]
    biases = jnp.zeros((2, size), f32)
    for g in range(groups):
        picked = [pick(total[26 + b * groups + g : 27 + b * groups + g], size, g * width) for b in range(BLOCKS)]
        biases = biases + jnp.concatenate(picked, axis=0)
    upb_ref[...] = biases


def pair_kernel(keep_ref, recv_ref, kept_ref, *sent_refs):
    kept_ref[...] = keep_ref[0].astype(f32) + recv_ref[0].astype(f32)
    for h, ref in enumerate(sent_refs):
        ref[...] = (keep_ref[h + 1].astype(f32) + recv_ref[h + 1].astype(f32)).astype(low)


def cross_kernel(count, kept_ref, *refs):
    recvs, outs, total_ref = refs[: len(refs) - count - 1], refs[len(refs) - count - 1 : -1], refs[-1]
    total = kept_ref[...]
    for ref in recvs:
        total = total + ref[...].astype(f32)
    total_ref[...] = total
    cut = kept_ref.shape[0] // count
    for d, ref in enumerate(outs):
        at = pl.multiple_of((lax.axis_index("seq") ^ d) * cut, cut)
        ref[...] = total_ref[pl.ds(at, cut), :].astype(ref.dtype)


def over_seq_kernel(*refs):
    small_ref, out_ref = refs[-2:]
    total = refs[0][...].astype(f32)
    for ref in refs[1:-2]:
        total = total + ref[...].astype(f32)
    cut = total.shape[0]
    out_ref[0:cut] = total.astype(low)
    small = small_ref[0].astype(f32)
    for i in range(1, small_ref.shape[0]):
        small = small + small_ref[i].astype(f32)
    out_ref[cut:] = small.astype(low)


def sum_kernel(*refs):
    total = refs[0][...].astype(f32)
    for ref in refs[1:-1]:
        total = total + ref[...].astype(f32)
    refs[-1][...] = total.astype(refs[-1].dtype)


def add_all(arrays, kind, name, after=(), us=0):
    return simple_call(sum_kernel, arrays, [(arrays[0].shape, kind)], name, after=after, us=us)[0]


def pair_stage(keep, recv, name, after=()):
    piece = keep.shape[1:]
    kept, *sent = simple_call(
        pair_kernel, [keep, recv], [(piece, f32)] + [(piece, low)] * (keep.shape[0] - 1), name, after=after, hbm=(0,), out_hbm=True
    )
    return kept, [swap(x, "dp", 2 * (h + 1)) for h, x in enumerate(sent)]


def summed_over(x, axis):
    bit = 1
    while bit < lax.axis_size(axis):
        x = x + swap(x, axis, bit)
        bit *= 2
    return x


def per_device(
    features,
    lengths,
    dw_weight,
    block_gains,
    block_biases,
    up_weight,
    up_bias,
    down_weight,
    head_gain,
    head_shift,
    head_weight,
    head_bias,
    audio_grad,
):
    count = lax.axis_size("dp")
    pairs = count // 2
    micro = features.shape[0]
    rows = features.shape[2]
    width = features.shape[3]
    units = up_weight.shape[2]
    ext = rows + 2 * HALO
    own = width // count
    size = units // count
    seq_count = lax.axis_size("seq")
    features = features[:, 0]
    audio_grad = audio_grad[:, 0]
    columns = 2 * HALF + EXTRA
    run = functools.partial(call, grid=micro, lengths=lengths)

    def edge(columns, at):
        return pl.BlockSpec((micro, HALO, columns), lambda i: (0, at, 0))

    last_at = rows // HALO - 1
    packed_ins = [
        dw_weight.swapaxes(0, 1),
        block_gains,
        block_biases.swapaxes(0, 1),
        up_bias,
        head_gain[None],
        head_shift[None],
        head_weight,
        up_weight,
        down_weight,
    ]
    packed_outs = [
        (micro, HALO, width + HOP),
        (micro, HALO, width + HOP),
        (16, HALF),
        (units // HALF * own + size + 3 * own, HALF),
    ]

    def whole_block(dims):
        return pl.BlockSpec(tuple(dims), lambda i: (0,) * len(dims))

    first, last, small_piece, rest_piece = pl.pallas_call(
        pack_kernel,
        grid=(1,),
        in_specs=[edge(width, 0), edge(width, last_at), edge(HOP, 0), edge(HOP, last_at)]
        + [whole_block(a.shape) for a in packed_ins],
        out_specs=[whole_block(dims) for dims in packed_outs],
        out_shape=[jax.ShapeDtypeStruct(dims, low) for dims in packed_outs],
        compiler_params=pltpu.CompilerParams(vmem_limit_bytes=60 * MiB),
        cost_estimate=cost(0),
        name="pack",
    )(features, features, audio_grad, audio_grad, *packed_ins)
    before = lax.ppermute(last, "seq", [(i, i + 1) for i in range(seq_count - 1)])
    after = lax.ppermute(first, "seq", [(i + 1, i) for i in range(seq_count - 1)])
    rest = lax.all_gather(rest_piece, "dp", axis=0)
    squared = jnp.asarray((window_values() ** 2).reshape(4, HOP), f32)
    tables = jnp.asarray(head_tables())

    def shape(columns):
        return (micro, ext, columns)

    def dma(*size):
        return pltpu.SemaphoreType.DMA(size or (count,))

    def across(x):
        return [x] + [swap(x, "dp", d) for d in range(2, count, 2)]

    grouped = units // HALF * own
    small_pieces = across(small_piece)
    small_even, block0_piece = simple_call(
        gather_first_kernel,
        small_pieces + [up_weight, down_weight],
        [((pairs, 16, HALF), low), ((grouped + size, HALF), low)],
        "stack_small",
        after=[before, after],
    )
    small_odd = swap(small_even, "dp", 1)
    block0_pieces = across(block0_piece)
    table_grad, recip = run(
        functools.partial(dft_kernel, rows),
        ins=[(before, "rows"), (audio_grad, "rows"), (after, "rows"), (squared, "all"), (tables, "all")],
        outs=[(shape(NFFT), low, "rows"), ((ext, HOP), f32, "all")],
        scratch=[],
        us=20,
        name="dft",
    )
    normed, unit, inv_std, masked, taps, vec, upb, bias_row_all = run(
        functools.partial(conv_kernel, rows, own, units),
        ins=[(before, "rows"), (features, "rows"), (after, "rows"), (head_bias[None], "all"), (small_even, "any"), (small_odd, "any")],
        after=[recip],
        outs=[
            (shape(width), low, "rows"),
            (shape(width), low, "rows"),
            (shape(1), f32, "rows"),
            (shape(width), low, "rows"),
            ((16, width), f32, "all"),
            ((16, width), f32, "all"),
            ((16, units), f32, "all"),
            ((1, columns), f32, "all"),
        ],
        scratch=[pltpu.VMEM((count, 16, 512), low), pltpu.VMEM((ext + 16, width), f32), dma()],
        name="conv",
    )
    (block0_even,) = simple_call(
        gather_kernel, block0_pieces, [((pairs, grouped + size, HALF), low)], "stack_block0", after=[taps]
    )
    block0 = [(block0_even, "any"), (swap(block0_even, "dp", 1), "any")]
    halves = (2 * micro, ext // 2)
    hidden, act, slope, branch = call(
        functools.partial(forward_kernel, own, size),
        2 * micro,
        lengths,
        ins=[
            (masked.reshape(halves + (width,)), "rows"),
            (normed.reshape(halves + (width,)), "rows"),
            (vec, "all"),
            (upb, "all"),
        ]
        + block0,
        outs=[
            (halves + (width,), f32, "rows"),
            (halves + (units,), low, "rows"),
            (halves + (units,), low, "rows"),
            (halves + (width,), low, "rows"),
        ],
        scratch=[pltpu.VMEM((width, units), low), pltpu.VMEM((units, width), low), dma(count, units // HALF), dma(count, 1)],
        name="forward",
    )
    hidden, act, slope, branch = (x.reshape(micro, ext, -1) for x in (hidden, act, slope, branch))
    packed = 3 * own + size + grouped
    audio, head_grad_rows, conv_grad1, keep1, send1, small_mid, sbias1 = run(
        functools.partial(middle_kernel, rows, own, size),
        ins=[
            (hidden, "rows"),
            (table_grad, "rows"),
            (recip, "all"),
            (taps, "all"),
            (vec, "all"),
            (upb, "all"),
            (bias_row_all, "all"),
            (tables, "any"),
            (rest, "any"),
        ],
        outs=[
            ((micro, rows, HOP), f32, "rows"),
            (shape(width), f32, "rows"),
            (shape(width), low, "rows"),
            ((pairs, packed, HALF), low, "all"),
            ((pairs, packed, HALF), low, "all"),
            ((16, width), f32, "all"),
            ((1, units), f32, "all"),
        ],
        scratch=[
            pltpu.VMEM((NFFT, NFFT), low),
            pltpu.VMEM((width, units), low),
            pltpu.VMEM((units, width), low),
            pltpu.VMEM((width, columns), low),
            pltpu.VMEM((width + 16, columns), f32),
            pltpu.VMEM((width + 16, units), f32),
            pltpu.VMEM((units, width), f32),
            pltpu.VMEM((ext, units), low),
            pltpu.VMEM((ext, units), low),
            pltpu.VMEM((ext + 16, width), f32),
            pltpu.VMEM((ext + 16, NFFT), f32),
            pltpu.VMEM((ext, width), f32),
            pltpu.VMEM((ext, width), f32),
            pltpu.VMEM((ext, 1), f32),
            pltpu.VMEM((ext, 1), f32),
            pltpu.VMEM((ext, width), low),
            pltpu.VMEM((ext, width), low),
            pltpu.VMEM((width + 16, rows), low),
            pltpu.VMEM((ext, width), low),
            pltpu.VMEM((ext, width), low),
            pltpu.VMEM((ext, NFFT), low),
            pltpu.VMEM((ext, columns), low),
            pltpu.VMEM((128, width), f32),
            dma(count, 5 + units // HALF),
        ],
        name="middle",
        limit=56,
    )
    kept1, recvs1 = pair_stage(keep1, swap(send1, "dp", 1), "late_pair")
    pre_grad, incoming, keep, send, small_down, sbias0 = run(
        functools.partial(back_down_kernel, rows, own, size),
        ins=[
            (head_grad_rows, "rows"),
            (conv_grad1, "rows"),
            (hidden, "rows"),
            (taps, "all"),
            (branch, "rows"),
            (act, "rows"),
            (slope, "rows"),
            (normed, "rows"),
            (vec, "all"),
        ]
        + block0,
        outs=[
            (shape(units), low, "rows"),
            (shape(width), f32, "rows"),
            ((pairs, grouped + size, width), low, "all"),
            ((pairs, grouped + size, width), low, "all"),
            ((16, width), f32, "all"),
            ((1, units), f32, "all"),
        ],
        scratch=[
            pltpu.VMEM((units, width), low),
            pltpu.VMEM((units, width), f32),
            pltpu.VMEM((width + 16, units), f32),
            pltpu.VMEM((ext, width), low),
            pltpu.VMEM((width + 16, rows), low),
            pltpu.VMEM((ext + 16, width), f32),
            pltpu.VMEM((128, width), f32),
            dma(count, 1),
        ],
        after=[kept1],
        us=20,
        name="back_down",
    )
    shard1 = add_all([kept1] + recvs1, low, "late_cross", after=[sbias0], us=200)
    late = lax.psum(shard1, "seq")
    kept, recvs = pair_stage(keep, swap(send, "dp", 1), "pair", after=[shard1])
    feature_grad, small_conv = run(
        functools.partial(back_up_kernel, rows, own),
        ins=[
            (pre_grad, "rows"),
            (unit, "rows"),
            (inv_std, "rows"),
            (features, "rows"),
            (incoming, "rows"),
            (taps, "all"),
            (vec, "all"),
        ]
        + block0,
        outs=[((micro, rows, width), f32, "rows"), ((16, width), f32, "all")],
        scratch=[pltpu.VMEM((width, units), low), pltpu.VMEM((ext + 16, width), f32), pltpu.VMEM((128, width), f32), dma(count, units // HALF)],
        after=[kept],
        name="back_up",
    )
    (smalls,) = simple_call(
        small_kernel, [small_conv, small_down, sbias0, small_mid, sbias1], [((SMALL, width), low)], "small"
    )
    cut = kept.shape[0] // seq_count
    small_all = lax.all_gather(smalls, "dp", axis=0)
    if cut % 16:
        own_sum = add_all([kept] + recvs, f32, "cross", after=[smalls])
        sent = own_sum.astype(low)
        whole = add_all([own_sum] + [swap(sent, "seq", d) for d in range(1, seq_count)], low, "over_seq")
        small = jnp.sum(small_all.astype(f32), axis=0).astype(low)
        small = add_all([small] + [swap(small, "seq", d) for d in range(1, seq_count)], low, "small_seq")
        parts = [jnp.concatenate([whole, small], axis=0)]
    else:
        pieces = simple_call(
            functools.partial(cross_kernel, seq_count),
            [kept] + recvs,
            [((cut, width), f32)] + [((cut, width), low)] * (seq_count - 1),
            "cross",
            scratch=[pltpu.VMEM(kept.shape, f32)],
            after=[smalls],
        )
        part = simple_call(
            over_seq_kernel,
            [pieces[0]] + [swap(pieces[d], "seq", d) for d in range(1, seq_count)] + [small_all],
            [((cut + SMALL, width), low)],
            "over_seq",
        )[0]
        parts = [part] + [swap(part, "seq", d) for d in range(1, seq_count)]
    outs = simple_call(
        functools.partial(final_kernel, own, size, len(parts)),
        [late] + parts,
        [
            ((BLOCKS, own, units), f32),
            ((BLOCKS, size, width), f32),
            ((own, 2 * BINS), f32),
            ((1, 2 * BINS), f32),
            ((KERNEL, BLOCKS, own), f32),
            ((BLOCKS, 2, own), f32),
            ((3, BLOCKS, own), f32),
            ((BLOCKS, size), f32),
            ((1, own), f32),
            ((1, own), f32),
        ],
        "final",
        scratch=[pltpu.VMEM(kept.shape, f32)],
    )
    up_grad, down_grad, head_grad, bias_grad, dw_grad, gains_grad, biases_grad, up_bias_grad, hgain_grad, hshift_grad = outs
    return (
        audio[:, None],
        feature_grad[:, None],
        dw_grad.swapaxes(0, 1),
        gains_grad,
        biases_grad.swapaxes(0, 1),
        up_grad,
        up_bias_grad,
        down_grad,
        hgain_grad[0],
        hshift_grad[0],
        head_grad,
        bias_grad[0],
    )


def solution(mesh):
    return jax.shard_map(
        per_device,
        mesh=mesh,
        in_specs=(
            P(None, "dp", "seq", None),
            P(None, "dp"),
            P(None, None, "dp"),
            P(None, None, "dp"),
            P(None, None, "dp"),
            P(None, "dp", None),
            P(None, "dp"),
            P(None, "dp", None),
            P("dp"),
            P("dp"),
            P("dp", None),
            P(),
            P(None, "dp", "seq", None),
        ),
        out_specs=(
            P(None, "dp", "seq", None),
            P(None, "dp", "seq", None),
            P(None, None, "dp"),
            P(None, None, "dp"),
            P(None, None, "dp"),
            P(None, "dp", None),
            P(None, "dp"),
            P(None, "dp", None),
            P("dp"),
            P("dp"),
            P("dp", None),
            P(),
        ),
        check_vma=False,
    )
```

```python
import functools
import math

import jax
import jax.numpy as jnp
import numpy as np
from jax import lax
from jax.experimental import pallas as pl
from jax.experimental.pallas import tpu as pltpu
from jax.sharding import PartitionSpec as P

NFFT = 1024
HOP = 256
BINS = 513
HALF = 512
EXTRA = 128
KERNEL = 7
BLOCKS = 2
HALO = 16
SMALL = 32
norm_eps = 1e-06
f32 = jnp.float32
low = jnp.bfloat16
rows_dims = (((0,), (0,)), ((), ()))
cols_dims = (((1,), (1,)), ((), ()))
MiB = 2**20
GELU = (0.7978202661111929, 0.03654664812915587, -0.00019444764679970054, -1.3688682486738934e-05)
SIN = (3.1415902835876266, -5.16740769757772, 2.544020809221036, -0.5594899050493729)
COS = (1.9999999069332557, -9.869585717340266, 8.116823828128622, -2.6637603211811274, 0.43939359457288596)


def window_values():
    return 0.5 - 0.5 * np.cos(np.arange(NFFT) * (2.0 * math.pi / NFFT))


def head_tables():
    row = np.arange(NFFT)
    frequency = np.where(row < HALF, row, np.where(row == HALF, HALF, row - HALF))
    angles = (frequency[:, None] * np.arange(NFFT)[None, :] % NFFT) * (2.0 * math.pi / NFFT)
    weight = np.where((row == 0) | (row == HALF), 1.0, 2.0)[:, None] / NFFT
    values = np.where((row <= HALF)[:, None], np.cos(angles), -np.sin(angles)) * weight
    return (values * window_values()[None, :]).astype(jnp.bfloat16)


def swap(x, axis, d):
    return lax.ppermute(x, axis, [(i, i ^ d) for i in range(lax.axis_size(axis))])


def poly(z, coefficients):
    p = coefficients[-1]
    for c in coefficients[-2::-1]:
        p = p * z + c
    return p


def gelu_parts(x):
    u = jnp.clip(x, -5.2, 5.2)
    z = u * u
    p = poly(z, [jnp.asarray(c, x.dtype) for c in GELU])
    half = jnp.asarray(0.5, x.dtype)
    cumulative = half * jnp.tanh(u * p) + half
    density = jnp.exp2(z * jnp.asarray(-0.5 * math.log2(math.e), x.dtype))
    return x * cumulative, cumulative + (x * jnp.asarray(1.0 / math.sqrt(2.0 * math.pi), x.dtype)) * density


def norm_parts(values):
    centred = values - jnp.mean(values, axis=1, keepdims=True)
    inv_std = lax.rsqrt(jnp.mean(centred * centred, axis=1, keepdims=True) + norm_eps)
    return centred * inv_std, inv_std


def norm_back(normed_grad, unit, inv_std, gain):
    unit_grad = normed_grad * gain
    inner = jnp.mean(unit_grad * unit, axis=1, keepdims=True)
    return inv_std * (unit_grad - jnp.mean(unit_grad, axis=1, keepdims=True) - unit * inner)


def total_rows(x):
    return jnp.sum(x, axis=0, keepdims=True)


def row(ref, i):
    return ref[i : i + 1]


def turns(x):
    r = x * (1.0 / (2.0 * math.pi))
    r = r - jnp.floor(r + 0.5)
    z = r * r
    half = r * poly(z, SIN)
    return 1.0 - 2.0 * (half * half), half * poly(z, COS)


class Frames:
    def __init__(self, rows, lengths_ref):
        self.rows = rows
        self.ext = rows + 2 * HALO
        self.own = slice(HALO, HALO + rows)
        self.start = lax.axis_index("seq") * rows - HALO
        self.total = rows * lax.axis_size("seq")
        self.length = lengths_ref[pl.program_id(0), 0]
        self.tiles = [(0, HALO)] + [(r, 64) for r in range(HALO, HALO + rows, 64)] + [(HALO + rows, HALO)]
        self.half = self.ext // 2

    def at(self, r=0, n=None):
        return lax.broadcasted_iota(jnp.int32, (n or self.ext, 1), 0) + (self.start + r)

    def inside(self, r=0, n=None):
        t = self.at(r, n)
        return (t >= 0) & (t < self.total)

    def mask(self, r=0, n=None):
        t = self.at(r, n)
        return (t >= 0) & (t < self.total) & (t < self.length)

    def owns(self, r):
        return HALO <= r < HALO + self.rows

    def parts(self):
        return [(r0, range(r0, r0 + self.half, 16)) for r0 in (0, self.half)]


def feature_tile(frames, before_ref, features_ref, after_ref, r, n):
    width = features_ref.shape[2]
    if r < HALO:
        tile = before_ref[0, r : r + n, :width]
    elif r < HALO + frames.rows:
        tile = features_ref[0, r - HALO : r - HALO + n]
    else:
        tile = after_ref[0, r - HALO - frames.rows : r - HALO - frames.rows + n, :width]
    return jnp.where(frames.mask(r, n), tile.astype(f32), 0.0)


def fold(x):
    total = x[0:8]
    for r in range(8, x.shape[0], 8):
        total = total + x[r : r + 8]
    return total


def add_to(ref, i, x):
    ref[8 * i : 8 * i + 8] += fold(x)


def assemble(even_ref, odd_ref, base, size, whole_ref, sems):
    me = lax.axis_index("dp")
    copies = []
    for h in range(even_ref.shape[0]):
        for c, ref in enumerate((even_ref, odd_ref)):
            at = pl.multiple_of((me ^ (2 * h + c)) * size, size)
            for g in range(whole_ref.shape[1] // HALF):
                copies.append(
                    pltpu.make_async_copy(
                        ref.at[h, pl.ds(base + g * size, size)],
                        whole_ref.at[pl.ds(at, size), pl.ds(g * HALF, HALF)],
                        sems.at[2 * h + c, g],
                    )
                )
    return copies


def run_copies(copies):
    for copy in copies:
        copy.start()
    for copy in copies:
        copy.wait()


def skipping(kernel, start, count):
    def inner(*refs):
        return kernel(*refs[:start], *refs[start + count :])

    return inner if count else kernel


def in_hbm(x):
    return pltpu.with_memory_space_constraint(x, pltpu.HBM)


def cost(us):
    return pl.CostEstimate(flops=1000 + int(us * 1e9), bytes_accessed=1000, transcendentals=0)


def call(kernel, grid, lengths, ins, outs, scratch, name, after=(), limit=48, us=0):
    def spec(shape, kind):
        if isinstance(kind, pl.BlockSpec):
            return kind
        if kind == "any":
            return pl.BlockSpec(memory_space=pl.ANY)
        if kind == "rows":
            return pl.BlockSpec((1,) + tuple(shape[1:]), lambda i, s: (i,) + (0,) * (len(shape) - 1))
        return pl.BlockSpec(tuple(shape), lambda i, s: (0,) * len(shape))

    kernel = skipping(kernel, 1 + len(ins), len(after))
    ins = ins + [(a, "any") for a in after]
    return pl.pallas_call(
        kernel,
        out_shape=[(pltpu.HBM if kind == "rows" or len(s) == 3 else jax.ShapeDtypeStruct)(tuple(s), d) for s, d, kind in outs],
        grid_spec=pltpu.PrefetchScalarGridSpec(
            num_scalar_prefetch=1,
            grid=(grid,),
            in_specs=[spec(a.shape, kind) for a, kind in ins],
            out_specs=[spec(s, kind) for s, _, kind in outs],
            scratch_shapes=scratch,
        ),
        compiler_params=pltpu.CompilerParams(vmem_limit_bytes=limit * MiB, dimension_semantics=("arbitrary",)),
        cost_estimate=cost(us),
        name=name,
    )(lengths, *[a if kind == "any" or a.shape[1] == HALO else in_hbm(a) for a, kind in ins])


def simple_call(kernel, ins, outs, name, scratch=(), after=(), limit=16, us=0, hbm=(), out_hbm=False):
    whole = pl.BlockSpec(memory_space=pltpu.VMEM)
    return pl.pallas_call(
        skipping(kernel, len(ins), len(after)),
        out_shape=[(pltpu.HBM if out_hbm else jax.ShapeDtypeStruct)(tuple(s), d) for s, d in outs],
        in_specs=[whole] * len(ins) + [pl.BlockSpec(memory_space=pl.ANY)] * len(after),
        out_specs=[whole] * len(outs),
        scratch_shapes=list(scratch),
        compiler_params=pltpu.CompilerParams(vmem_limit_bytes=limit * MiB),
        cost_estimate=cost(us),
        name=name,
    )(*[in_hbm(a) if i in hbm else a for i, a in enumerate(ins)], *after)


def head_columns(x):
    lane = lax.broadcasted_iota(jnp.int32, (x.shape[0], EXTRA), 1)
    tail = jnp.where(lane == 0, x[:, BINS - 1 : BINS], jnp.where(lane == 1, x[:, 2 * BINS - 1 :], 0.0))
    return x[:, : BINS - 1], x[:, BINS : 2 * BINS - 1], tail


def pack_kernel(
    first_ref, last_ref, gfirst_ref, glast_ref, dw_ref, gains_ref, biases_ref, upb_ref, hgain_ref, hshift_ref,
    head_ref, up_ref, down_ref, first_out, last_out, small_out, rest_out,
):
    width = first_ref.shape[2]
    first_out[:, :, :width] = first_ref[...]
    first_out[:, :, width:] = gfirst_ref[...].astype(low)
    last_out[:, :, :width] = last_ref[...]
    last_out[:, :, width:] = glast_ref[...].astype(low)
    own = up_ref.shape[1]
    small_out[...] = jnp.zeros(small_out.shape, low)

    def stack(parts):
        parts = [p.astype(f32) for p in parts]
        filled = sum(p.shape[0] for p in parts)
        return jnp.concatenate(parts + [jnp.zeros((16 - filled, parts[0].shape[1]), f32)], axis=0).astype(low)

    def halves(x):
        high = x.astype(low).astype(f32)
        return [high, x - high]

    small_out[:, 0:own] = stack([dw_ref[:, 0, :], dw_ref[:, 1, :]])
    small_out[:, 128 : 128 + own] = stack(
        [gains_ref[0], gains_ref[1], biases_ref[:, 0, :], biases_ref[:, 1, :]] + halves(hgain_ref[...]) + halves(hshift_ref[...])
    )
    small_out[:, 256 : 256 + upb_ref.shape[1]] = stack([upb_ref[...]])
    size = down_ref.shape[1]
    base = up_ref.shape[2] // HALF * own
    for g in range(0, up_ref.shape[2], HALF):
        rest_out[g // HALF * own : (g // HALF + 1) * own] = up_ref[1, :, g : g + HALF]
    rest_out[base : base + size] = down_ref[1]
    size = base + size

    magnitude, phase, tail = head_columns(head_ref[...])
    rest_out[size : size + own] = magnitude.astype(low)
    rest_out[size + own : size + 2 * own] = phase.astype(low)
    rest_out[size + 2 * own :] = jnp.zeros((own, HALF), low)
    rest_out[size + 2 * own :, :EXTRA] = tail.astype(low)


def dft_kernel(rows, lengths, before_ref, grad_ref, after_ref, squared_ref, table_ref, out_ref, recip_ref):
    frames = Frames(rows, lengths)
    width = before_ref.shape[2] - HOP

    @pl.when(pl.program_id(0) == 0)
    def _():
        envelope = jnp.zeros((frames.ext, HOP), f32)
        for q in range(4):
            source = frames.at() + (2 - q)
            valid = (source >= 0) & (source < frames.total)
            envelope = envelope + jnp.where(valid, row(squared_ref, q), 0.0)
        recip_ref[...] = jnp.where(frames.inside(), 1.0 / envelope, 0.0)

    whole = jnp.concatenate(
        [before_ref[0, :, width:].astype(f32), grad_ref[0], after_ref[0, :, width:].astype(f32)], axis=0
    )
    own = jnp.where(frames.mask(), whole * recip_ref[...], 0.0)
    parts = [own if q == 2 else pltpu.roll(own, (2 - q) % frames.ext, 0) for q in range(4)]
    framed = jnp.where(frames.inside(), jnp.concatenate(parts, axis=1), 0.0).astype(low)
    out_ref[0] = lax.dot_general(framed, table_ref[...], cols_dims, preferred_element_type=f32).astype(low)


def put_padded(pad_ref, frames, tile_of):
    zeros = jnp.zeros((8, pad_ref.shape[1]), f32)
    pad_ref[0:8] = zeros
    pad_ref[frames.ext + 8 :] = zeros
    for r, n in frames.tiles:
        pad_ref[8 + r : 8 + r + n] = tile_of(r, n)


def conv_tile(pad_ref, r, n, taps_ref, base, bias):
    window = pad_ref[r : r + n + 16]
    conv = bias + row(taps_ref, base + 3) * window[8 : 8 + n]
    for k in range(KERNEL):
        if k != 3:
            conv = conv + row(taps_ref, base + k) * pltpu.roll(window, (3 - k) % (n + 16), 0)[8 : 8 + n]
    return conv


def conv_norm(frames, pad_ref, taps_ref, base, vec_ref, b, unit_at, inv_at, normed_at):
    for r, n in frames.tiles:
        unit, inv_std = norm_parts(conv_tile(pad_ref, r, n, taps_ref, base, bias_row(vec_ref, b, 0)))
        unit_at[r : r + n] = unit.astype(unit_at.dtype)
        inv_at[r : r + n] = inv_std
        normed_at[r : r + n] = (unit * gain_row(vec_ref, b, 0) + bias_row(vec_ref, b, 1)).astype(low)


def gain_row(ref, b, i):
    return row(ref, 2 * b + i)


def bias_row(ref, b, i):
    return row(ref, 4 + 3 * b + i)


def conv_kernel(
    rows, own, units, lengths, before_ref, features_ref, after_ref, hbias_ref, even_ref, odd_ref,
    normed_ref, unit_ref, inv_ref, masked_ref, taps_ref, vec_ref, upb_ref, bias_ref, small_ref, pad_ref, sems,
):
    @pl.when(pl.program_id(0) == 0)
    def _():
        me = lax.axis_index("dp")
        count = 2 * even_ref.shape[0]
        copies = []
        for d in range(count):
            ref = odd_ref if d % 2 else even_ref
            copies.append(
                pltpu.make_async_copy(ref.at[d // 2], small_ref.at[d], sems.at[d])
            )
        run_copies(copies)

        def spread(lanes, size, out_ref):
            total = jnp.zeros(out_ref.shape, f32)
            at = lax.broadcasted_iota(jnp.int32, (size, out_ref.shape[1]), 0)
            to = lax.broadcasted_iota(jnp.int32, (size, out_ref.shape[1]), 1)
            for d in range(count):
                place = jnp.where(to == at + (me ^ d) * size, 1.0, 0.0).astype(low)
                total = total + jnp.dot(small_ref[d, :, lanes : lanes + size], place, preferred_element_type=f32)
            out_ref[...] = total

        spread(0, own, taps_ref)
        spread(128, own, vec_ref)
        spread(256, units // count, upb_ref)
        magnitude, phase, tail = head_columns(hbias_ref[...])
        bias_ref[:, :HALF] = magnitude
        bias_ref[:, HALF : 2 * HALF] = phase
        bias_ref[:, 2 * HALF :] = tail

    frames = Frames(rows, lengths)
    put_padded(pad_ref, frames, functools.partial(feature_tile, frames, before_ref, features_ref, after_ref))
    masked_ref[0] = pad_ref[8 : 8 + frames.ext].astype(low)
    conv_norm(frames, pad_ref, taps_ref, 0, vec_ref, 0, unit_ref.at[0], inv_ref.at[0], normed_ref.at[0])


def gelu_rows(normed, weight_ref, bias, act_at, slope_at, rows, chunk=256):
    for c in range(0, weight_ref.shape[1], chunk):
        pre = jnp.dot(normed, weight_ref[:, c : c + chunk], preferred_element_type=f32) + bias[:, c : c + chunk]
        act, slope = gelu_parts(pre.astype(low))
        act_at[rows, c : c + chunk] = act
        slope_at[rows, c : c + chunk] = slope


def up_gelu(frames, normed_at, weight_ref, bias, act_at, slope_at):
    for r0, _ in frames.parts():
        part = slice(r0, r0 + frames.half)
        gelu_rows(normed_at[part], weight_ref, bias, act_at, slope_at, part)


def forward_kernel(
    own, size, lengths, masked_ref, normed_ref, vec_ref, upb_ref, even_ref, odd_ref,
    hidden_ref, act_ref, slope_ref, branch_ref, up_ref, down_ref, sems, sems2,
):
    first = pl.program_id(0) == 0
    ups = assemble(even_ref, odd_ref, 0, own, up_ref, sems)
    downs = assemble(even_ref, odd_ref, up_ref.shape[1] // HALF * own, size, down_ref, sems2)

    @pl.when(first)
    def _():
        for copy in ups + downs:
            copy.start()
        for copy in ups:
            copy.wait()

    act_at = act_ref.at[0]
    gelu_rows(normed_ref[0], up_ref, row(upb_ref, 0), act_at, slope_ref.at[0], slice(0, act_at.shape[0]))

    @pl.when(first)
    def _():
        for copy in downs:
            copy.wait()

    product = jnp.dot(act_at[...], down_ref[...], preferred_element_type=f32)
    for r in range(0, product.shape[0], 16):
        branch = product[r : r + 16] + bias_row(vec_ref, 0, 2)
        branch_ref[0, r : r + 16] = branch.astype(low)
        hidden_ref[0, r : r + 16] = masked_ref[0, r : r + 16].astype(f32) + gain_row(vec_ref, 0, 1) * branch


def split_rows(total_at, size, keep_at, send_at, pieces):
    me = lax.axis_index("dp")
    for h in range(pieces):
        at = pl.multiple_of((me ^ (2 * h)) * size, size)
        keep_at(h, total_at(pl.ds(at, size)).astype(low))
        at = pl.multiple_of((me ^ (2 * h + 1)) * size, size)
        send_at(h, total_at(pl.ds(at, size)).astype(low))


def give(ref, base):
    def put(h, value):
        ref[h, base : base + value.shape[0], : value.shape[1]] = value

    return put


def split_columns(total_ref, base, size, keep_ref, send_ref):
    for g in range(0, total_ref.shape[1], HALF):
        stop = min(g + HALF, total_ref.shape[1])
        at = base + g // HALF * size
        split_rows(lambda r: total_ref[r, g:stop], size, give(keep_ref, at), give(send_ref, at), keep_ref.shape[0])


def branch_tile(frames, r, hgrad, branch, gain, bgrad_at, sums_ref, at):
    bgrad = (gain * hgrad).astype(low)
    bgrad_at[r : r + 16] = bgrad
    if frames.owns(r):
        add_to(sums_ref, at, hgrad * branch.astype(f32))
        add_to(sums_ref, at + 1, bgrad.astype(f32))


def back_down(frames, bgrad_at, act_at, slope_at, weight_ref, total_ref, pgrad_at, chunk=512):
    own = frames.own
    for c in range(0, weight_ref.shape[0], chunk):
        part = slice(c, c + chunk)
        for r0, tiles in frames.parts():
            act_grad = lax.dot_general(bgrad_at[r0 : r0 + frames.half], weight_ref[part], cols_dims, preferred_element_type=f32)
            for r in tiles:
                grad = (act_grad[r - r0 : r - r0 + 16] * slope_at[r : r + 16, part].astype(f32)).astype(low)
                pgrad_at[r : r + 16, part] = grad
        total_ref[part] += lax.dot_general(act_at[own, part], bgrad_at[own], rows_dims, preferred_element_type=f32)


def back_up_norm(frames, pgrad_at, unit_at, inv_at, gain, weight_ref, put, sums_ref):
    for r0, tiles in frames.parts():
        product = lax.dot_general(pgrad_at[r0 : r0 + frames.half], weight_ref[...], cols_dims, preferred_element_type=f32)
        for r in tiles:
            normed_grad = product[r - r0 : r - r0 + 16]
            unit = unit_at[r : r + 16].astype(f32)
            conv_grad = norm_back(normed_grad, unit, inv_at[r : r + 16], gain)
            if frames.owns(r):
                conv_grad = conv_grad.astype(low).astype(f32)
                add_to(sums_ref, 7, conv_grad)
                add_to(sums_ref, 8, normed_grad * unit)
                add_to(sums_ref, 9, normed_grad)
            else:
                conv_grad = jnp.where(frames.inside(r, 16), conv_grad, 0.0).astype(low).astype(f32)
            put(r, conv_grad)


def conv_back_tile(frames, r, n, pad_ref, block_in_of, hgrad, taps_ref, base, sums_ref):
    window = pad_ref[r : r + n + 16]
    owns = frames.owns(r)
    block_in = block_in_of(r, n) if owns else None
    for k in range(KERNEL):
        moved = (window if k == 3 else pltpu.roll(window, (k - 3) % (n + 16), 0))[8 : 8 + n]
        hgrad = hgrad + row(taps_ref, base + k) * moved
        if owns:
            add_to(sums_ref, k, block_in * moved)
    return hgrad


def close_sums(sums_ref, small_ref):
    for i in range(sums_ref.shape[0] // 8):
        small_ref[i : i + 1] = total_rows(sums_ref[8 * i : 8 * i + 8])


def middle_kernel(
    rows, own, size, lengths, h_ref, tgrad_ref, recip_ref, taps_ref, vec_ref, upb_ref, bias_ref,
    table_hbm, rest_ref,
    audio_ref, hgrad_ref, cgrad_ref, keep_ref, send_ref, small_ref, sbias_ref,
    table_ref, up_ref, down_ref, head_ref, head_total, up_total, down_total, act_ref, slope_ref,
    pad_ref, frame_ref, unit1_ref, unit2_ref, inv1_ref, inv2_ref, normed1_ref, normed2_ref, turned_ref,
    branch_ref, bgrad_ref, spectrum_ref, lgrad_ref, sums_ref, sems,
):
    step = pl.program_id(0)

    copies = []
    groups = up_ref.shape[1] // HALF
    width = up_ref.shape[0]
    places = [(g * own, own, up_ref, g * HALF, HALF) for g in range(groups)]
    places.append((groups * own, size, down_ref, 0, HALF))
    base = groups * own + size
    places += [(base + g * own, own, head_ref, g * HALF, lanes) for g, lanes in enumerate((HALF, HALF, EXTRA))]
    for j in range(rest_ref.shape[0]):
        for i, (at, many, ref, lane, lanes) in enumerate(places):
            copy = pltpu.make_async_copy(
                rest_ref.at[j, pl.ds(at, many), pl.ds(0, lanes)],
                ref.at[pl.ds(j * many, many), pl.ds(lane, lanes)],
                sems.at[j, i],
            )
            copies.append((copy, i))
    copies.append((pltpu.make_async_copy(table_hbm, table_ref, sems.at[0, len(places)]), len(places)))
    copies.sort(key=lambda pair: pair[1])

    @pl.when(step == 0)
    def _():
        for copy, _ in copies:
            copy.start()
        for ref in (head_total, up_total, down_total, sums_ref):
            ref[...] = jnp.zeros_like(ref)
        turned_ref[width:] = jnp.ones((16, rows), low)
        for copy, _ in copies:
            copy.wait()

    frames = Frames(rows, lengths)
    mine, half, ext = frames.own, frames.half, frames.ext

    def block_in_tile(r, n):
        return jnp.where(frames.inside(r, n), h_ref[0, r : r + n], 0.0).astype(low).astype(f32)

    put_padded(pad_ref, frames, block_in_tile)
    conv_norm(frames, pad_ref, taps_ref, KERNEL, vec_ref, 1, unit1_ref, inv1_ref, normed1_ref)
    up_gelu(frames, normed1_ref, up_ref, row(upb_ref, 1), act_ref, slope_ref)

    head_gain = row(vec_ref, 10) + row(vec_ref, 11)
    head_shift = row(vec_ref, 12) + row(vec_ref, 13)
    for r0, tiles in frames.parts():
        product = jnp.dot(act_ref[r0 : r0 + half], down_ref[...], preferred_element_type=f32)
        for r in tiles:
            branch = product[r - r0 : r - r0 + 16] + bias_row(vec_ref, 1, 2)
            branch_ref[r : r + 16] = branch.astype(low)
            unit, inv_std = norm_parts(h_ref[0, r : r + 16] + gain_row(vec_ref, 1, 1) * branch)
            unit2_ref[r : r + 16] = unit
            inv2_ref[r : r + 16] = inv_std
            normed2_ref[r : r + 16] = (unit * head_gain + head_shift).astype(low)

    lane = lax.broadcasted_iota(jnp.int32, (16, EXTRA), 1)
    for r0, tiles in frames.parts():
        product = jnp.dot(normed2_ref[r0 : r0 + half], head_ref[...], preferred_element_type=f32)
        for r in tiles:
            logits = product[r - r0 : r - r0 + 16] + bias_ref[...]
            magnitude = jnp.exp(logits[:, :HALF])
            cos, sin = turns(logits[:, HALF : 2 * HALF])
            re = magnitude * cos
            im = magnitude * sin
            last = logits[:, 2 * HALF :]
            cos, sin = turns(pltpu.roll(last, EXTRA - 1, 1))
            top = jnp.exp(jnp.where(lane == 0, last, 0.0))
            top_re = top * cos
            top_im = top * sin
            re = re.astype(low)
            spectrum_ref[r : r + 16, :HALF] = re
            spectrum_ref[r : r + 16, HALF : HALF + EXTRA] = jnp.where(lane == 0, top_re, im[:, :EXTRA]).astype(low)
            im = im.astype(low)
            spectrum_ref[r : r + 16, HALF + EXTRA :] = im[:, EXTRA:]
            re_grad = tgrad_ref[0, r : r + 16, :HALF]
            top_grad = tgrad_ref[0, r : r + 16, HALF : HALF + EXTRA].astype(f32)
            im_first = jnp.where(lane == 0, 0.0, top_grad).astype(low)
            im_grad = jnp.concatenate([im_first, tgrad_ref[0, r : r + 16, HALF + EXTRA :]], axis=1)
            log_last = jnp.where(lane == 0, top_grad * top_re, 0.0)
            phase_last = jnp.where(lane == 1, pltpu.roll(top_grad * top_im, 1, 1), 0.0)
            grads = (re_grad * re + im_grad * im, im_grad * re - re_grad * im, log_last - phase_last)
            for g, grad in enumerate(grads):
                part = slice(g * HALF, g * HALF + grad.shape[1])
                lgrad_ref[r : r + 16, part] = grad.astype(low)

    for r0, tiles in frames.parts():
        product = jnp.dot(spectrum_ref[r0 : r0 + half], table_ref[...], preferred_element_type=f32)
        for r in tiles:
            framed = product[r - r0 : r - r0 + 16]
            if not frames.owns(r):
                framed = jnp.where(frames.inside(r, 16), framed, 0.0)
            frame_ref[8 + r : 8 + r + 16] = framed

    hgrad_at = hgrad_ref.at[0]
    for r0, tiles in frames.parts():
        product = lax.dot_general(lgrad_ref[r0 : r0 + half], head_ref[...], cols_dims, preferred_element_type=f32)
        for r in tiles:
            normed_grad = product[r - r0 : r - r0 + 16]
            unit = unit2_ref[r : r + 16]
            hgrad = norm_back(normed_grad, unit, inv2_ref[r : r + 16], head_gain)
            hgrad_at[r : r + 16] = hgrad
            if frames.owns(r):
                add_to(sums_ref, 12, normed_grad * unit)
                add_to(sums_ref, 13, normed_grad)
            branch_tile(frames, r, hgrad, branch_ref[r : r + 16], gain_row(vec_ref, 1, 1), bgrad_ref, sums_ref, 10)

    def audio_tile(r, n):
        audio = frame_ref[8 + r : 8 + r + n, 2 * HOP : 3 * HOP]
        for q in (0, 1, 3):
            window = frame_ref[r : r + n + 16, q * HOP : (q + 1) * HOP]
            audio = audio + pltpu.roll(window, (q - 2) % (n + 16), 0)[8 : 8 + n]
        audio_ref[0, r - HALO : r - HALO + n] = jnp.where(frames.mask(r, n), audio * recip_ref[r : r + n], 0.0)

    def beside(chunks, tiles, dot_of, put, work):
        each = -(-len(tiles) // len(chunks))
        for i, part in enumerate(chunks):
            product = dot_of(part)
            for r, n in tiles[i * each : (i + 1) * each]:
                work(r, n)
            put(part, product)

    own_tiles = [tile for tile in frames.tiles if frames.owns(tile[0])]
    turned_ref[:width] = normed2_ref[mine].T

    def put_head(part, product):
        head_total[:, part] += product

    beside(
        [slice(c, c + 384) for c in range(0, head_total.shape[1], 384)],
        own_tiles,
        lambda part: jnp.dot(turned_ref[...], lgrad_ref[mine, part], preferred_element_type=f32),
        put_head,
        audio_tile,
    )

    back_down(frames, bgrad_ref, act_ref, slope_ref, down_ref, down_total, slope_ref)
    def put_conv(r, grad):
        cgrad_ref[0, r : r + 16] = grad.astype(low)

    back_up_norm(frames, slope_ref, unit1_ref, inv1_ref, gain_row(vec_ref, 1, 0), up_ref, put_conv, sums_ref)
    turned_ref[:width] = normed1_ref[mine].T

    for c in range(0, up_total.shape[1], 256):
        up_total[:, c : c + 256] += jnp.dot(turned_ref[...], slope_ref[mine, c : c + 256], preferred_element_type=f32)

    @pl.when(step == pl.num_programs(0) - 1)
    def _():
        close_sums(sums_ref, small_ref)
        sbias_ref[...] = up_total[width : width + 1]
        groups = up_ref.shape[1] // HALF * own
        split_columns(up_total, 0, own, keep_ref, send_ref)
        split_columns(down_total, groups, size, keep_ref, send_ref)
        base = groups + size
        bias = head_total[width : width + 1]
        block = jnp.concatenate([bias[:, g : g + 384] for g in (0, 384, 768)] + [jnp.zeros((13, 384), f32)], axis=0)
        for h in range(keep_ref.shape[0]):
            for ref in (keep_ref, send_ref):
                ref[h, base + 2 * own :] = jnp.zeros((own, HALF), low)
                ref[h, base + 2 * own : base + 2 * own + 16, EXTRA:] = block.astype(low)
        split_columns(head_total, base, own, keep_ref, send_ref)


def back_down_kernel(
    rows, own, size, lengths, head_ref, cgrad_ref, h_ref, taps_ref, branch_ref, act_ref, slope_ref, normed_ref, vec_ref,
    even_ref, odd_ref, pgrad_ref, hgrad_ref, keep_ref, send_ref, small_ref, sbias_ref, weight_ref, down_total, up_total, bgrad_ref, turned_ref, pad_ref, sums_ref, sems,
):
    step = pl.program_id(0)

    @pl.when(step == 0)
    def _():
        copies = assemble(even_ref, odd_ref, up_total.shape[1] // HALF * own, size, weight_ref, sems)
        for copy in copies:
            copy.start()
        for ref in (down_total, up_total, sums_ref):
            ref[...] = jnp.zeros_like(ref)
        turned_ref[normed_ref.shape[2] :] = jnp.ones((16, rows), low)
        for copy in copies:
            copy.wait()

    frames = Frames(rows, lengths)
    mine = frames.own
    put_padded(pad_ref, frames, lambda r, n: cgrad_ref[0, r : r + n].astype(f32))

    def block_in_tile(r, n):
        return jnp.where(frames.inside(r, n), h_ref[0, r : r + n], 0.0).astype(low).astype(f32)

    for r, n in frames.tiles:
        hgrad_ref[0, r : r + n] = conv_back_tile(
            frames, r, n, pad_ref, block_in_tile, head_ref[0, r : r + n], taps_ref, KERNEL, sums_ref
        )
    for r in range(0, frames.ext, 16):
        branch_tile(frames, r, hgrad_ref[0, r : r + 16], branch_ref[0, r : r + 16], gain_row(vec_ref, 0, 1), bgrad_ref, sums_ref, 8)
    back_down(frames, bgrad_ref, act_ref.at[0], slope_ref.at[0], weight_ref, down_total, pgrad_ref.at[0])
    width = normed_ref.shape[2]
    turned_ref[:width] = normed_ref[0, mine].T
    up_total[...] += jnp.dot(turned_ref[...], pgrad_ref[0, mine], preferred_element_type=f32)

    @pl.when(step == pl.num_programs(0) - 1)
    def _():
        close_sums(sums_ref, small_ref)
        sbias_ref[...] = up_total[width : width + 1]
        split_columns(up_total, 0, own, keep_ref, send_ref)
        split_columns(down_total, up_total.shape[1] // HALF * own, size, keep_ref, send_ref)


def back_up_kernel(
    rows, own, lengths, pgrad_ref, unit_ref, inv_ref, features_ref, hgrad_ref, taps_ref, vec_ref, even_ref, odd_ref,
    out_ref, small_ref, weight_ref, pad_ref, sums_ref, sems,
):
    step = pl.program_id(0)

    @pl.when(step == 0)
    def _():
        sums_ref[...] = jnp.zeros_like(sums_ref)
        run_copies(assemble(even_ref, odd_ref, 0, own, weight_ref, sems))

    frames = Frames(rows, lengths)
    zeros = jnp.zeros((8, pad_ref.shape[1]), f32)
    pad_ref[0:8] = zeros
    pad_ref[frames.ext + 8 :] = zeros

    def put_conv(r, grad):
        pad_ref[8 + r : 8 + r + 16] = grad

    back_up_norm(
        frames, pgrad_ref.at[0], unit_ref.at[0], inv_ref.at[0], gain_row(vec_ref, 0, 0), weight_ref, put_conv, sums_ref
    )

    def block_in_tile(r, n):
        return jnp.where(frames.mask(r, n), features_ref[0, r - HALO : r - HALO + n].astype(f32), 0.0)

    for r, n in frames.tiles:
        if frames.owns(r):
            hgrad = conv_back_tile(frames, r, n, pad_ref, block_in_tile, hgrad_ref[0, r : r + n], taps_ref, 0, sums_ref)
            out_ref[0, r - HALO : r - HALO + n] = jnp.where(frames.mask(r, n), hgrad, 0.0)

    @pl.when(step == pl.num_programs(0) - 1)
    def _():
        close_sums(sums_ref, small_ref)


def small_kernel(conv0_ref, down0_ref, bias0_ref, mid_ref, bias1_ref, out_ref):
    width = out_ref.shape[1]
    groups = [r[:, g : g + width] for r in (bias0_ref, bias1_ref) for g in range(0, r.shape[1], width)]
    rows = [
        conv0_ref[0:7], down0_ref[0:7],
        conv0_ref[8:9], down0_ref[8:9], mid_ref[8:9], mid_ref[10:11],
        conv0_ref[7:8], conv0_ref[9:10], down0_ref[9:10], mid_ref[7:8], mid_ref[9:10], mid_ref[11:12],
        mid_ref[12:14],
    ] + groups
    filled = 26 + len(groups)
    rows = rows + [jnp.zeros((out_ref.shape[0] - filled, width), f32)] * (filled < out_ref.shape[0])
    out_ref[...] = jnp.concatenate(rows, axis=0).astype(low)


def gather_kernel(*refs):
    for h, ref in enumerate(refs[:-1]):
        refs[-1][h] = ref[...]


def gather_first_kernel(*refs):
    up_ref, down_ref, stack_ref, piece_ref = refs[-4:]
    for h, ref in enumerate(refs[:-4]):
        stack_ref[h] = ref[...]
    own = up_ref.shape[1]
    for g in range(0, up_ref.shape[2], HALF):
        piece_ref[g // HALF * own : (g // HALF + 1) * own] = up_ref[0, :, g : g + HALF]
    piece_ref[up_ref.shape[2] // HALF * own :] = down_ref[0]


def final_kernel(
    own, size, parts, late_ref, *refs,
):
    part_refs = refs[:parts]
    up_ref, down_ref, head_ref, hbias_ref, dw_ref, gains_ref, biases_ref, upb_ref, hgain_ref, hshift_ref, rows_ref = refs[parts:]
    total = 0.0
    for d, ref in enumerate(part_refs):
        cut = ref.shape[0] - SMALL
        total = total + ref[cut:].astype(f32)
        at = 0 if parts == 1 else pl.multiple_of((lax.axis_index("seq") ^ d) * cut, cut)
        rows_ref[pl.ds(at, cut), :] = ref[0:cut].astype(f32)
    groups = up_ref.shape[2] // HALF
    base = groups * own + size
    late = late_ref[...].astype(f32)
    for g in range(groups):
        up_ref[0, :, g * HALF : (g + 1) * HALF] = rows_ref[g * own : (g + 1) * own]
        up_ref[1, :, g * HALF : (g + 1) * HALF] = late[g * own : (g + 1) * own]
    down_ref[0] = rows_ref[groups * own : base]
    down_ref[1] = late[groups * own : base]

    def joined(magnitude, phase, tail):
        return jnp.concatenate([magnitude, tail[:, 0:1], phase, tail[:, 1:2]], axis=1)

    tail = late[base + 2 * own :]
    head_ref[...] = joined(late[base : base + own], late[base + own : base + 2 * own], tail)
    bias = jnp.concatenate([tail[g : g + 1, EXTRA:] for g in range(3)], axis=1)
    hbias_ref[...] = joined(bias[:, :HALF], bias[:, HALF : 2 * HALF], bias[:, 2 * HALF :])

    width = total.shape[1]
    me = lax.axis_index("dp")

    def pick(values, count, base):
        at = lax.broadcasted_iota(jnp.int32, (width, count), 0)
        to = lax.broadcasted_iota(jnp.int32, (width, count), 1)
        place = jnp.where(at + base == to + me * count, 1.0, 0.0).astype(low)
        high = values.astype(low)
        rest = (values - high.astype(f32)).astype(low)
        return jnp.dot(high, place, preferred_element_type=f32) + jnp.dot(rest, place, preferred_element_type=f32)

    rows = pick(total[0:32], own, 0)
    for b in range(BLOCKS):
        dw_ref[:, b, :] = rows[KERNEL * b : KERNEL * (b + 1)]
        gains_ref[b] = rows[14 + 2 * b : 16 + 2 * b]
        biases_ref[:, b, :] = rows[18 + 3 * b : 21 + 3 * b]
    hgain_ref[...] = rows[24:25]
    hshift_ref[...] = rows[25:26]
    biases = jnp.zeros((2, size), f32)
    for g in range(groups):
        picked = [pick(total[26 + b * groups + g : 27 + b * groups + g], size, g * width) for b in range(BLOCKS)]
        biases = biases + jnp.concatenate(picked, axis=0)
    upb_ref[...] = biases


def pair_kernel(keep_ref, recv_ref, kept_ref, *sent_refs):
    kept_ref[...] = keep_ref[0].astype(f32) + recv_ref[0].astype(f32)
    for h, ref in enumerate(sent_refs):
        ref[...] = (keep_ref[h + 1].astype(f32) + recv_ref[h + 1].astype(f32)).astype(low)


def cross_kernel(count, kept_ref, *refs):
    recvs, outs, total_ref = refs[: len(refs) - count - 1], refs[len(refs) - count - 1 : -1], refs[-1]
    total = kept_ref[...]
    for ref in recvs:
        total = total + ref[...].astype(f32)
    total_ref[...] = total
    cut = kept_ref.shape[0] // count
    for d, ref in enumerate(outs):
        at = pl.multiple_of((lax.axis_index("seq") ^ d) * cut, cut)
        ref[...] = total_ref[pl.ds(at, cut), :].astype(ref.dtype)


def over_seq_kernel(*refs):
    small_ref, out_ref = refs[-2:]
    total = refs[0][...].astype(f32)
    for ref in refs[1:-2]:
        total = total + ref[...].astype(f32)
    cut = total.shape[0]
    out_ref[0:cut] = total.astype(low)
    small = small_ref[0].astype(f32)
    for i in range(1, small_ref.shape[0]):
        small = small + small_ref[i].astype(f32)
    out_ref[cut:] = small.astype(low)


def sum_kernel(*refs):
    total = refs[0][...].astype(f32)
    for ref in refs[1:-1]:
        total = total + ref[...].astype(f32)
    refs[-1][...] = total.astype(refs[-1].dtype)


def add_all(arrays, kind, name, after=(), us=0):
    return simple_call(sum_kernel, arrays, [(arrays[0].shape, kind)], name, after=after, us=us)[0]


def pair_stage(keep, recv, name, after=()):
    piece = keep.shape[1:]
    kept, *sent = simple_call(
        pair_kernel, [keep, recv], [(piece, f32)] + [(piece, low)] * (keep.shape[0] - 1), name, after=after, hbm=(0,), out_hbm=True
    )
    return kept, [swap(x, "dp", 2 * (h + 1)) for h, x in enumerate(sent)]


def summed_over(x, axis):
    bit = 1
    while bit < lax.axis_size(axis):
        x = x + swap(x, axis, bit)
        bit *= 2
    return x


def per_device(
    features,
    lengths,
    dw_weight,
    block_gains,
    block_biases,
    up_weight,
    up_bias,
    down_weight,
    head_gain,
    head_shift,
    head_weight,
    head_bias,
    audio_grad,
):
    count = lax.axis_size("dp")
    pairs = count // 2
    micro = features.shape[0]
    rows = features.shape[2]
    width = features.shape[3]
    units = up_weight.shape[2]
    ext = rows + 2 * HALO
    own = width // count
    size = units // count
    seq_count = lax.axis_size("seq")
    features = features[:, 0]
    audio_grad = audio_grad[:, 0]
    columns = 2 * HALF + EXTRA
    run = functools.partial(call, grid=micro, lengths=lengths)

    def edge(columns, at):
        return pl.BlockSpec((micro, HALO, columns), lambda i: (0, at, 0))

    last_at = rows // HALO - 1
    packed_ins = [
        dw_weight.swapaxes(0, 1),
        block_gains,
        block_biases.swapaxes(0, 1),
        up_bias,
        head_gain[None],
        head_shift[None],
        head_weight,
        up_weight,
        down_weight,
    ]
    packed_outs = [
        (micro, HALO, width + HOP),
        (micro, HALO, width + HOP),
        (16, HALF),
        (units // HALF * own + size + 3 * own, HALF),
    ]

    def whole_block(dims):
        return pl.BlockSpec(tuple(dims), lambda i: (0,) * len(dims))

    first, last, small_piece, rest_piece = pl.pallas_call(
        pack_kernel,
        grid=(1,),
        in_specs=[edge(width, 0), edge(width, last_at), edge(HOP, 0), edge(HOP, last_at)]
        + [whole_block(a.shape) for a in packed_ins],
        out_specs=[whole_block(dims) for dims in packed_outs],
        out_shape=[jax.ShapeDtypeStruct(dims, low) for dims in packed_outs],
        compiler_params=pltpu.CompilerParams(vmem_limit_bytes=60 * MiB),
        cost_estimate=cost(0),
        name="pack",
    )(features, features, audio_grad, audio_grad, *packed_ins)
    before = lax.ppermute(last, "seq", [(i, i + 1) for i in range(seq_count - 1)])
    after = lax.ppermute(first, "seq", [(i + 1, i) for i in range(seq_count - 1)])
    rest = lax.all_gather(rest_piece, "dp", axis=0)
    squared = jnp.asarray((window_values() ** 2).reshape(4, HOP), f32)
    tables = jnp.asarray(head_tables())

    def shape(columns):
        return (micro, ext, columns)

    def dma(*size):
        return pltpu.SemaphoreType.DMA(size or (count,))

    def across(x):
        return [x] + [swap(x, "dp", d) for d in range(2, count, 2)]

    grouped = units // HALF * own
    small_pieces = across(small_piece)
    small_even, block0_piece = simple_call(
        gather_first_kernel,
        small_pieces + [up_weight, down_weight],
        [((pairs, 16, HALF), low), ((grouped + size, HALF), low)],
        "stack_small",
        after=[before, after],
    )
    small_odd = swap(small_even, "dp", 1)
    block0_pieces = across(block0_piece)
    table_grad, recip = run(
        functools.partial(dft_kernel, rows),
        ins=[(before, "rows"), (audio_grad, "rows"), (after, "rows"), (squared, "all"), (tables, "all")],
        outs=[(shape(NFFT), low, "rows"), ((ext, HOP), f32, "all")],
        scratch=[],
        us=20,
        name="dft",
    )
    normed, unit, inv_std, masked, taps, vec, upb, bias_row_all = run(
        functools.partial(conv_kernel, rows, own, units),
        ins=[(before, "rows"), (features, "rows"), (after, "rows"), (head_bias[None], "all"), (small_even, "any"), (small_odd, "any")],
        after=[recip],
        outs=[
            (shape(width), low, "rows"),
            (shape(width), low, "rows"),
            (shape(1), f32, "rows"),
            (shape(width), low, "rows"),
            ((16, width), f32, "all"),
            ((16, width), f32, "all"),
            ((16, units), f32, "all"),
            ((1, columns), f32, "all"),
        ],
        scratch=[pltpu.VMEM((count, 16, 512), low), pltpu.VMEM((ext + 16, width), f32), dma()],
        name="conv",
    )
    (block0_even,) = simple_call(
        gather_kernel, block0_pieces, [((pairs, grouped + size, HALF), low)], "stack_block0", after=[taps]
    )
    block0 = [(block0_even, "any"), (swap(block0_even, "dp", 1), "any")]
    halves = (2 * micro, ext // 2)
    hidden, act, slope, branch = call(
        functools.partial(forward_kernel, own, size),
        2 * micro,
        lengths,
        ins=[
            (masked.reshape(halves + (width,)), "rows"),
            (normed.reshape(halves + (width,)), "rows"),
            (vec, "all"),
            (upb, "all"),
        ]
        + block0,
        outs=[
            (halves + (width,), f32, "rows"),
            (halves + (units,), low, "rows"),
            (halves + (units,), low, "rows"),
            (halves + (width,), low, "rows"),
        ],
        scratch=[pltpu.VMEM((width, units), low), pltpu.VMEM((units, width), low), dma(count, units // HALF), dma(count, 1)],
        name="forward",
        limit=60,
    )
    hidden, act, slope, branch = (x.reshape(micro, ext, -1) for x in (hidden, act, slope, branch))
    packed = 3 * own + size + grouped
    audio, head_grad_rows, conv_grad1, keep1, send1, small_mid, sbias1 = run(
        functools.partial(middle_kernel, rows, own, size),
        ins=[
            (hidden, "rows"),
            (table_grad, "rows"),
            (recip, "all"),
            (taps, "all"),
            (vec, "all"),
            (upb, "all"),
            (bias_row_all, "all"),
            (tables, "any"),
            (rest, "any"),
        ],
        outs=[
            ((micro, rows, HOP), f32, "rows"),
            (shape(width), f32, "rows"),
            (shape(width), low, "rows"),
            ((pairs, packed, HALF), low, "all"),
            ((pairs, packed, HALF), low, "all"),
            ((16, width), f32, "all"),
            ((1, units), f32, "all"),
        ],
        scratch=[
            pltpu.VMEM((NFFT, NFFT), low),
            pltpu.VMEM((width, units), low),
            pltpu.VMEM((units, width), low),
            pltpu.VMEM((width, columns), low),
            pltpu.VMEM((width + 16, columns), f32),
            pltpu.VMEM((width + 16, units), f32),
            pltpu.VMEM((units, width), f32),
            pltpu.VMEM((ext, units), low),
            pltpu.VMEM((ext, units), low),
            pltpu.VMEM((ext + 16, width), f32),
            pltpu.VMEM((ext + 16, NFFT), f32),
            pltpu.VMEM((ext, width), f32),
            pltpu.VMEM((ext, width), f32),
            pltpu.VMEM((ext, 1), f32),
            pltpu.VMEM((ext, 1), f32),
            pltpu.VMEM((ext, width), low),
            pltpu.VMEM((ext, width), low),
            pltpu.VMEM((width + 16, rows), low),
            pltpu.VMEM((ext, width), low),
            pltpu.VMEM((ext, width), low),
            pltpu.VMEM((ext, NFFT), low),
            pltpu.VMEM((ext, columns), low),
            pltpu.VMEM((128, width), f32),
            dma(count, 5 + units // HALF),
        ],
        name="middle",
        limit=56,
    )
    kept1, recvs1 = pair_stage(keep1, swap(send1, "dp", 1), "late_pair")
    pre_grad, incoming, keep, send, small_down, sbias0 = run(
        functools.partial(back_down_kernel, rows, own, size),
        ins=[
            (head_grad_rows, "rows"),
            (conv_grad1, "rows"),
            (hidden, "rows"),
            (taps, "all"),
            (branch, "rows"),
            (act, "rows"),
            (slope, "rows"),
            (normed, "rows"),
            (vec, "all"),
        ]
        + block0,
        outs=[
            (shape(units), low, "rows"),
            (shape(width), f32, "rows"),
            ((pairs, grouped + size, width), low, "all"),
            ((pairs, grouped + size, width), low, "all"),
            ((16, width), f32, "all"),
            ((1, units), f32, "all"),
        ],
        scratch=[
            pltpu.VMEM((units, width), low),
            pltpu.VMEM((units, width), f32),
            pltpu.VMEM((width + 16, units), f32),
            pltpu.VMEM((ext, width), low),
            pltpu.VMEM((width + 16, rows), low),
            pltpu.VMEM((ext + 16, width), f32),
            pltpu.VMEM((128, width), f32),
            dma(count, 1),
        ],
        after=[kept1],
        us=20,
        name="back_down",
        limit=60,
    )
    shard1 = add_all([kept1] + recvs1, low, "late_cross", after=[sbias0], us=200)
    late = lax.psum(shard1, "seq")
    kept, recvs = pair_stage(keep, swap(send, "dp", 1), "pair", after=[shard1])
    feature_grad, small_conv = run(
        functools.partial(back_up_kernel, rows, own),
        ins=[
            (pre_grad, "rows"),
            (unit, "rows"),
            (inv_std, "rows"),
            (features, "rows"),
            (incoming, "rows"),
            (taps, "all"),
            (vec, "all"),
        ]
        + block0,
        outs=[((micro, rows, width), f32, "rows"), ((16, width), f32, "all")],
        scratch=[pltpu.VMEM((width, units), low), pltpu.VMEM((ext + 16, width), f32), pltpu.VMEM((128, width), f32), dma(count, units // HALF)],
        after=[kept],
        name="back_up",
        limit=60,
    )
    (smalls,) = simple_call(
        small_kernel, [small_conv, small_down, sbias0, small_mid, sbias1], [((SMALL, width), low)], "small"
    )
    cut = kept.shape[0] // seq_count
    small_all = lax.all_gather(smalls, "dp", axis=0)
    if cut % 16:
        own_sum = add_all([kept] + recvs, f32, "cross", after=[smalls])
        sent = own_sum.astype(low)
        whole = add_all([own_sum] + [swap(sent, "seq", d) for d in range(1, seq_count)], low, "over_seq")
        small = jnp.sum(small_all.astype(f32), axis=0).astype(low)
        small = add_all([small] + [swap(small, "seq", d) for d in range(1, seq_count)], low, "small_seq")
        parts = [jnp.concatenate([whole, small], axis=0)]
    else:
        pieces = simple_call(
            functools.partial(cross_kernel, seq_count),
            [kept] + recvs,
            [((cut, width), f32)] + [((cut, width), low)] * (seq_count - 1),
            "cross",
            scratch=[pltpu.VMEM(kept.shape, f32)],
            after=[smalls],
        )
        part = simple_call(
            over_seq_kernel,
            [pieces[0]] + [swap(pieces[d], "seq", d) for d in range(1, seq_count)] + [small_all],
            [((cut + SMALL, width), low)],
            "over_seq",
        )[0]
        parts = [part] + [swap(part, "seq", d) for d in range(1, seq_count)]
    outs = simple_call(
        functools.partial(final_kernel, own, size, len(parts)),
        [late] + parts,
        [
            ((BLOCKS, own, units), f32),
            ((BLOCKS, size, width), f32),
            ((own, 2 * BINS), f32),
            ((1, 2 * BINS), f32),
            ((KERNEL, BLOCKS, own), f32),
            ((BLOCKS, 2, own), f32),
            ((3, BLOCKS, own), f32),
            ((BLOCKS, size), f32),
            ((1, own), f32),
            ((1, own), f32),
        ],
        "final",
        scratch=[pltpu.VMEM(kept.shape, f32)],
    )
    up_grad, down_grad, head_grad, bias_grad, dw_grad, gains_grad, biases_grad, up_bias_grad, hgain_grad, hshift_grad = outs
    return (
        audio[:, None],
        feature_grad[:, None],
        dw_grad.swapaxes(0, 1),
        gains_grad,
        biases_grad.swapaxes(0, 1),
        up_grad,
        up_bias_grad,
        down_grad,
        hgain_grad[0],
        hshift_grad[0],
        head_grad,
        bias_grad[0],
    )


def solution(mesh):
    return jax.shard_map(
        per_device,
        mesh=mesh,
        in_specs=(
            P(None, "dp", "seq", None),
            P(None, "dp"),
            P(None, None, "dp"),
            P(None, None, "dp"),
            P(None, None, "dp"),
            P(None, "dp", None),
            P(None, "dp"),
            P(None, "dp", None),
            P("dp"),
            P("dp"),
            P("dp", None),
            P(),
            P(None, "dp", "seq", None),
        ),
        out_specs=(
            P(None, "dp", "seq", None),
            P(None, "dp", "seq", None),
            P(None, None, "dp"),
            P(None, None, "dp"),
            P(None, None, "dp"),
            P(None, "dp", None),
            P(None, "dp"),
            P(None, "dp", None),
            P("dp"),
            P("dp"),
            P("dp", None),
            P(),
        ),
        check_vma=False,
    )
```
